32 devices in a mesh: groups: 2 (over x), dp: 2 (over core), tensor: 8 (over z, y).
Axes of the slice: x: 2, y: 2, z: 4, core: 2. Of those that a mesh axis runs over, the one named last changes fastest.
Arguments:
- tokens: bfloat16 [1024, 8192], P(('groups', 'dp'), 'tensor'), parts along dimension 0, may hold values from -6 to 6
- cotangent: bfloat16 [1024, 8192], P(('groups', 'dp'), 'tensor'), parts along dimension 0, may hold values from -6 to 6
- gate_weight: bfloat16 [8192, 14336], P(None, 'tensor'), may hold values from -0.09375 to 0.09375
- up_weight: bfloat16 [8192, 14336], P(None, 'tensor'), may hold values from -0.0625 to 0.0625
- down_matrix_frozen: bfloat16 [14336, 8192], P('tensor'), may hold values from -0.046875 to 0.046875
- adapter_a: bfloat16 [32, 14336, 64], P('groups', 'tensor'), parts along dimension 0, may hold values from -0.046875 to 0.046875
- adapter_b: bfloat16 [32, 64, 8192], P('groups', None, 'tensor'), parts along dimension 0, may hold values from -0.75 to 0.75
- tenant: int32 [8], P(('groups', 'dp')), parts along dimension 0, may hold values from 0 to 15
- ranks: int32 [32], P('groups'), parts along dimension 0, may hold values from 8 to 64
Outputs:
- grad_input: bfloat16 [1024, 8192], P(('groups', 'dp'), 'tensor'), parts along dimension 0
- grad_a: float32 [32, 14336, 64], P('groups', 'tensor'), parts along dimension 0
- grad_b: float32 [32, 64, 8192], P('groups', None, 'tensor'), parts along dimension 0
The draws below stay inside these ranges and needn't reach their ends.
There are 2 independent parts, one for each index of `groups`. The reference program is written for one: setup_inputs(seed, part) draws one part's arguments, and reference() takes and returns one part's arrays. A program takes and returns all parts, laid end to end along the dimension named above; an argument that names none is the same for every part. Nothing has to cross between parts.
Inputs may be any that keep to these rules, and one draw needn't show every extreme that they name: Each tenant's adapter uses only its first ranks[t] of 64 rank columns; blocks are labelled independently, so tenants hold uneven numbers of blocks. Every block of 128 tokens belongs to one tenant.
All inputs are finite; a program needn't handle non-finite values.
Results may differ from the reference program's by a relative error of at most 0.0065.
Values may be sent and summed in bfloat16 or wider, within the bound.
No kernel may reach another device: no remote copies, remote signals or barrier semaphores. Data moves between devices by JAX's collectives and lax.ppermute only.
A program may use at most 256 MiB of HBM per device.

```python
import jax
import jax.numpy as jnp

D = 8192
HIDDEN_UNITS = 14336
TENANTS = 16
R = 64
BLOCK = 128
NBLK = 4
TOKEN_TOTAL = 512


def place_ends(values, stream_key, least, largest):
    index_at = [jax.random.randint(jax.random.fold_in(stream_key, axis), (), 0, length) for axis, length in enumerate(values.shape)]
    main_axis = values.shape.index(max(values.shape))
    beside = index_at[:main_axis] + [(index_at[main_axis] + 1) % values.shape[main_axis]] + index_at[main_axis + 1:]
    return values.at[tuple(index_at)].set(least).at[tuple(beside)].set(largest)


def strengthened(result, own_key, source, target, parts, factor):
    owner, partner = [(jnp.arange(result.shape[axis_at]) // (result.shape[axis_at] // parts)).reshape([-1 if axis == axis_at else 1 for axis in range(result.ndim)]) for axis_at in (source, target)]
    chosen = jax.random.permutation(own_key, parts)[partner]
    strong = (owner == chosen) | (owner == (partner + parts // 2) % parts)
    return jnp.where(strong, factor * result, result)


def block_scale(stream_key, shape, shards, smallest, high):
    level = 1.0
    for axis_at, shards_of in shards:
        steps = jax.random.uniform(jax.random.fold_in(jax.random.fold_in(stream_key, 6), axis_at), (shards_of,), jnp.float32, smallest / len(shards), high / len(shards))
        level = level * jnp.repeat(jnp.exp(steps), shape[axis_at] // shards_of).reshape((-1,) + (1,) * (len(shape) - 1 - axis_at))
    return level


def scatter_about(own_key, dims, spread, bound, cuts=(), kind=jnp.bfloat16):
    factor_of = block_scale(own_key, dims, cuts, -0.22, 0.18) if cuts else 1.0
    values = jax.random.normal(own_key, dims, jnp.float32) * spread * factor_of
    return jnp.minimum(jnp.maximum(values, -bound), bound).astype(kind)


def bell_draw_with(key, dims, scale, most, cuts, heavy, kind=jnp.bfloat16):
    drawn = scale * jax.random.normal(key, dims, jnp.float32)
    if cuts:
        drawn = drawn * block_scale(key, dims, cuts, -0.22, 0.18)
    return jnp.clip(strengthened(drawn, jax.random.fold_in(key, 3), *heavy), -most, most).astype(kind)


def setup_inputs(seed: int = 0, part: int = 0) -> dict:
    arg_keys = jax.random.split(jax.random.key(seed), 10)
    own_keys = jax.random.split(jax.random.fold_in(arg_keys[9], part), 10)
    tokens = scatter_about(own_keys[0], (TOKEN_TOTAL, D), 1.0, 6.0, ((0, 2), (1, 8)))
    cotangent = scatter_about(own_keys[1], (TOKEN_TOTAL, D), 1.0, 6.0, ((0, 2), (1, 8)))
    gate_weight = bell_draw_with(arg_keys[2], (D, HIDDEN_UNITS), D ** -0.5, 0.09375, ((1, 8),), (1, 0, 8, 2.0))
    up_weight = scatter_about(arg_keys[3], (D, HIDDEN_UNITS), D ** -0.5, 0.0625, ((1, 8),))
    down_matrix_frozen = scatter_about(arg_keys[4], (HIDDEN_UNITS, D), HIDDEN_UNITS ** -0.5, 0.046875, ((0, 8),))
    adapter_a = scatter_about(own_keys[5], (TENANTS, HIDDEN_UNITS, R), HIDDEN_UNITS ** -0.5, 0.046875, ((1, 8),))
    adapter_b = scatter_about(own_keys[6], (TENANTS, R, D), R ** -0.5, 0.75, ((2, 8),))
    tenant = place_ends(jax.random.randint(own_keys[7], (NBLK,), 0, TENANTS), jax.random.fold_in(own_keys[7], 1), 0, TENANTS - 1).astype(jnp.int32)
    ranks = place_ends(jax.random.randint(own_keys[8], (TENANTS,), R // 8, R + 1), jax.random.fold_in(own_keys[8], 1), R // 8, R).astype(jnp.int32)
    return {"tokens": tokens, "cotangent": cotangent, "gate_weight": gate_weight, "up_weight": up_weight, "down_matrix_frozen": down_matrix_frozen, "adapter_a": adapter_a, "adapter_b": adapter_b, "tenant": tenant, "ranks": ranks}


adapter_alpha_factor = 32.0


def reference(tokens, cotangent, gate_weight, up_weight, down_matrix_frozen, adapter_a, adapter_b, tenant, ranks):
    gate_pre = jnp.dot(tokens, gate_weight, preferred_element_type=jnp.float32)
    up_pre = jnp.dot(tokens, up_weight, preferred_element_type=jnp.float32)
    hidden = (jax.nn.silu(gate_pre) * up_pre).astype(jnp.bfloat16)
    mask_table = (jnp.arange(R, dtype=jnp.int32)[None, :] < ranks[:, None]).astype(jnp.float32)
    tenant_scale_lookup = adapter_alpha_factor / ranks.astype(jnp.float32)
    selected_down_adapter = adapter_a[tenant].astype(jnp.float32)
    b_chosen = adapter_b[tenant].astype(jnp.float32)
    mask_chosen = mask_table[tenant]
    scale_chosen = tenant_scale_lookup[tenant]
    hid_blocks = hidden.reshape(NBLK, BLOCK, HIDDEN_UNITS).astype(jnp.float32)
    cot_blocks = cotangent.reshape(NBLK, BLOCK, D).astype(jnp.float32)
    low_sum = jnp.einsum('bnf,bfr->bnr', hid_blocks, selected_down_adapter) * mask_chosen[:, None, :]
    back_sum = jnp.einsum('bnd,brd->bnr', cot_blocks, b_chosen) * mask_chosen[:, None, :]
    low_bf = low_sum.astype(jnp.bfloat16).astype(jnp.float32)
    backward_half_precision = (scale_chosen[:, None, None] * back_sum).astype(jnp.bfloat16).astype(jnp.float32)
    adapter_gradient_term = jnp.einsum('gpl,gdl->gpd', backward_half_precision, selected_down_adapter).reshape(TOKEN_TOTAL, HIDDEN_UNITS)
    hidden_gradient = jnp.dot(cotangent, down_matrix_frozen.T, preferred_element_type=jnp.float32) + adapter_gradient_term
    onehot = (tenant[:, None] == jnp.arange(TENANTS, dtype=jnp.int32)[None, :]).astype(jnp.float32)
    block_a = jnp.einsum('bnf,bnr->bfr', hid_blocks, backward_half_precision)
    grad_a = jnp.einsum('bt,bfr->tfr', onehot, block_a)
    block_b = jnp.einsum('bnr,bnd->brd', low_bf, cot_blocks)
    grad_b = tenant_scale_lookup[:, None, None] * jnp.einsum('bt,brd->trd', onehot, block_b)
    sigma_gate = jax.nn.sigmoid(gate_pre)
    grad_gate = (hidden_gradient * up_pre * sigma_gate * (1.0 + gate_pre * (1.0 - sigma_gate))).astype(jnp.bfloat16)
    grad_up = (hidden_gradient * gate_pre * sigma_gate).astype(jnp.bfloat16)
    grad_input = jnp.dot(grad_gate, gate_weight.T, preferred_element_type=jnp.float32)
    grad_input = grad_input + jnp.dot(grad_up, up_weight.T, preferred_element_type=jnp.float32)
    return grad_input.astype(jnp.bfloat16), grad_a, grad_b
```

```python
import functools

import jax
import jax.numpy as jnp
from jax import lax
from jax.experimental import pallas as pl
from jax.experimental.pallas import tpu as pltpu
from jax.sharding import PartitionSpec as P

adapter_alpha_factor = 32.0
f32 = jnp.float32
bf16 = jnp.bfloat16
together = lax.optimization_barrier

RING_PLAN = (
    ("T10", "T00"),
    ("C10", "C00"),
    ("T20", "T10"),
    ("C20", "C10"),
    ("T30", "T20"),
    ("C30", "C20"),
    ("C21", "C11"),
)
PAIR_PLAN = (
    ("T01", "T00"),
    ("C01", "C00"),
    ("T11", "T10"),
    ("C11", "C10"),
    ("T21", "T20"),
    ("T31", "T30"),
    ("C31", "C30"),
)
RING, PAIR = 4, 2


def contract_trailing_axis(left, right):
    return lax.dot_general(
        left, right, (((1,), (1,)), ((), ())), preferred_element_type=f32
    )


ANYWHERE = pl.BlockSpec(memory_space=pl.ANY)
NEAR = pl.BlockSpec(memory_space=pltpu.VMEM)
SCALARS = pl.BlockSpec(memory_space=pltpu.SMEM)
MARK = jax.ShapeDtypeStruct((8, 128), f32)


def cost(flops, weights):
    return pl.CostEstimate(flops=flops, bytes_accessed=weights, transcendentals=0)


def in_hbm(value):
    return pltpu.with_memory_space_constraint(value, pltpu.HBM)


def call(body, name, mark, scalars, far, out_shape, scratch, vmem, estimate):
    def marked(*refs):
        refs, (mark_ref, *scratch_refs) = refs[1 : ends + 1], refs[ends + 1 :]
        mark_ref[...] = jnp.zeros_like(mark_ref)
        body(*refs, *scratch_refs)

    ends = len(scalars) + len(far) + len(out_shape)
    return pl.pallas_call(
        marked,
        in_specs=[ANYWHERE] + [SCALARS] * len(scalars) + [ANYWHERE] * len(far),
        out_specs=[ANYWHERE] * len(out_shape) + [NEAR],
        out_shape=[*out_shape, MARK],
        scratch_shapes=scratch,
        compiler_params=pltpu.CompilerParams(vmem_limit_bytes=vmem << 20),
        cost_estimate=estimate,
        name=name,
    )(mark, *scalars, *far)


def at(index, size):
    return pl.ds(pl.multiple_of(index * size, size), size)


class Flow:
    def __init__(self, far, close, sems, out=False):
        self.far, self.close, self.sems, self.out = far, close, sems, out
        self.slots = sems.shape[0]

    def copy(self, n):
        ends = (self.close(n), self.far(n)) if self.out else (self.far(n), self.close(n))
        return pltpu.make_async_copy(*ends, self.sems.at[lax.rem(n, self.slots)])

    def start(self, n):
        self.copy(n).start()

    def wait(self, n):
        self.copy(n).wait()


def tiles(steps, inward, *phases):
    most = max([f.slots for f in inward])
    for n in range(most):
        for f in inward:
            if n < min(f.slots, steps):
                f.start(n)
    share = steps // len(phases)
    for p, (outward, compute) in enumerate(phases):

        def step(k, carry, base=p * share, outward=outward, compute=compute):
            n = base + k
            for f in inward:
                f.wait(n)
            for f in outward:

                @pl.when(k >= f.slots)
                def _():
                    f.wait(k - f.slots)

            compute(n, [f.close(n) for f in inward], [f.close(k) for f in outward])
            for f in outward:
                f.start(k)
            for f in inward:

                @pl.when(n + f.slots < steps)
                def _():
                    f.start(n + f.slots)

            return carry

        lax.fori_loop(0, share, step, 0)
    for outward, _ in phases:
        for f in outward:
            for k in range(max(0, share - f.slots), share):
                f.wait(k)


def buffers(slots, *shapes):
    out = []
    for shape, dtype in shapes:
        out += [pltpu.VMEM((slots, *shape), dtype), pltpu.SemaphoreType.DMA((slots,))]
    return out


def flows(fars, scratch, out=False):
    made = []
    for i, far in enumerate(fars):
        buffer, sems = scratch[2 * i : 2 * i + 2]
        made.append(Flow(far, lambda n, b=buffer: b.at[lax.rem(n, b.shape[0])], sems, out))
    return made


class Refs:
    def __init__(self, refs):
        self.refs = list(refs)

    def __call__(self, count):
        got, self.refs = self.refs[:count], self.refs[count:]
        return got


def gate_up(mark, chunks, places, gate, up, sums, low=None, tile=256, slots=3):
    count = len(chunks)
    rows, depth = chunks[0].shape
    hid = gate.shape[1]
    blocks = 0 if low is None else low[0].shape[0]
    length = 0 if low is None else rows // blocks
    rank = 0 if low is None else low[1].shape[1]
    scalars = [places] + ([] if low is None else [low[0]])
    far = [*chunks, in_hbm(gate), in_hbm(up)] + ([] if sums is None else [in_hbm(t) for t in sums])
    far += [] if low is None else [low[1]]
    types = [f32, f32] if low is None else [f32, f32, bf16]
    outs = [pltpu.HBM((rows, hid), t) for t in types]
    if low is not None:
        outs += [jax.ShapeDtypeStruct((blocks, length, rank), f32)]
    scratch = buffers(1, *[((rows, depth), bf16)] * count)
    scratch += buffers(slots, *[((depth, tile), bf16)] * (2 * count))
    scratch += buffers(slots, *[((rows, tile), f32)] * (0 if sums is None else 2))
    scratch += buffers(2, *[((rank, tile), bf16)] * blocks)
    scratch += buffers(2, *[((rows, tile), t) for t in types])
    scratch += [] if low is None else buffers(1, ((blocks, length, rank), f32))

    def body(*refs):
        take = Refs(refs)
        (where,) = take(1)
        label = take(1)[0] if low is not None else None
        x_far = take(count)
        weights = take(2)
        sums_far = take(0 if sums is None else 2)
        adapter = take(0 if low is None else 1)
        out_far = take(len(types))
        low_far = take(0 if low is None else 1)
        x = flows([lambda n, r=r: r for r in x_far], take(2 * count))
        w = flows(
            [
                lambda n, r=r, c=c: r.at[at(where[c], depth), at(n, tile)]
                for r in weights
                for c in range(count)
            ],
            take(4 * count),
        )
        w += flows([lambda n, r=r: r.at[:, at(n, tile)] for r in sums_far], take(2 * len(sums_far)))
        w += flows(
            [lambda n, b=b: adapter[0].at[label[b], :, at(n, tile)] for b in range(blocks)],
            take(2 * blocks),
        )
        o = flows([lambda n, r=r: r.at[:, at(n, tile)] for r in out_far], take(2 * len(out_far)), True)
        l = flows([lambda n, r=r: r for r in low_far], take(2 * len(low_far)), True)
        for f in x:
            f.start(0)
        for f in l:
            f.close(0)[...] = jnp.zeros((blocks, length, rank), f32)

        def compute(n, got, put):
            @pl.when(n == 0)
            def _():
                for f in x:
                    f.wait(0)

            found = []
            for which in range(2):
                total = None if sums is None else got[2 * count + which][...]
                for c in range(count):
                    term = jnp.dot(
                        x[c].close(0)[...], got[which * count + c][...], preferred_element_type=f32
                    )
                    total = term if total is None else total + term
                found.append(total)
            if low is None:
                put[0][...], put[1][...] = found
                return
            gate_pre, up_pre = found
            sigma = jax.nn.sigmoid(gate_pre)
            act = gate_pre * sigma
            put[0][...] = act
            put[1][...] = up_pre * sigma * (1.0 + gate_pre * (1.0 - sigma))
            hidden = (act * up_pre).astype(bf16)
            put[2][...] = hidden
            for b in range(blocks):
                l[0].close(0)[b] += contract_trailing_axis(
                    hidden[b * length : (b + 1) * length], got[len(got) - blocks + b][...]
                )

        tiles(hid // tile, w, (o, compute))
        for f in l:
            f.start(0)
            f.wait(0)

    work = count * rows * depth * hid
    estimate = cost(4 * work, 4 * work // rows)
    return call(body, "gate_up", mark, scalars, far, outs, scratch, 32, estimate)


def down_back(mark, chunks, rows, places, down, total, last=None, tile=256, slots=4):
    count = len(chunks)
    depth = chunks[0].shape[1]
    hid = down.shape[0]
    blocks = 0 if last is None else last[0].shape[0]
    length = 0 if last is None else rows // blocks
    rank = 0 if last is None else last[1].shape[1]
    scalars = [places] + ([] if last is None else [last[0]])
    far = [*chunks, in_hbm(down)] + ([] if total is None else [in_hbm(total)])
    far += [] if last is None else [*last[1:3], in_hbm(last[3]), in_hbm(last[4])]
    types = [f32] if last is None else [bf16, bf16]
    scratch = buffers(1, *[((rows, depth), bf16)] * count)
    scratch += buffers(slots, *[((tile, depth), bf16)] * count)
    scratch += [] if total is None else buffers(slots, ((rows, tile), f32))
    if last is not None:
        scratch += buffers(1, ((blocks, length, rank), bf16))
        scratch += buffers(slots, *[((rank, tile), bf16)] * blocks)
        scratch += buffers(slots, *[((rows, tile), f32)] * 2)
    scratch += buffers(2, *[((rows, tile), t) for t in types])

    def body(*refs):
        take = Refs(refs)
        (where,) = take(1)
        label = take(1)[0] if last is not None else None
        x_far = take(count)
        (weight,) = take(1)
        total_far = take(0 if total is None else 1)
        adapter, back_far = take(0 if last is None else 2) or (None, None)
        factors = take(0 if last is None else 2)
        out_far = take(len(types))
        x = flows([lambda n, r=r: r.at[0:rows] for r in x_far], take(2 * count))
        w = flows(
            [lambda n, c=c: weight.at[at(n, tile), at(where[c], depth)] for c in range(count)],
            take(2 * count),
        )
        w += flows([lambda n, r=r: r.at[:, at(n, tile)] for r in total_far], take(2 * len(total_far)))
        if last is not None:
            x += flows([lambda n: back_far], take(2))
        w += flows(
            [lambda n, b=b: adapter.at[label[b], :, at(n, tile)] for b in range(blocks)],
            take(2 * blocks),
        )
        w += flows([lambda n, r=r: r.at[:, at(n, tile)] for r in factors], take(2 * len(factors)))
        o = flows([lambda n, r=r: r.at[:, at(n, tile)] for r in out_far], take(2 * len(out_far)), True)
        for f in x:
            f.start(0)

        def compute(n, got, put):
            @pl.when(n == 0)
            def _():
                for f in x:
                    f.wait(0)

            value = None if total is None else got[count][...]
            for c in range(count):
                term = contract_trailing_axis(x[c].close(0)[...], got[c][...])
                value = term if value is None else value + term
            if last is None:
                put[0][...] = value
                return
            *adapters, act, slope = got[len(got) - blocks - 2 :]
            for b in range(blocks):
                span = slice(b * length, (b + 1) * length)
                grad = value[span] + jnp.dot(
                    x[count].close(0)[b], adapters[b][...], preferred_element_type=f32
                )
                put[0][span] = (grad * slope[span]).astype(bf16)
                put[1][span] = (grad * act[span]).astype(bf16)

        tiles(hid // tile, w, (o, compute))

    if last is None:
        outs = [pltpu.HBM((rows, hid), f32)]
    else:
        outs = [jax.ShapeDtypeStruct((rows, hid), bf16)] * 2
    work = count * rows * depth * hid
    estimate = cost(2 * work, 2 * work // rows)
    return call(body, "down_back", mark, scalars, far, outs, scratch, 24, estimate)


def input_parts(mark, places, grads, gate, up, width, dtypes, tile=256, slots=4):
    rows, hid = grads[0].shape
    count = len(dtypes)
    share = width // tile
    scratch = buffers(1, *[((rows, hid), bf16)] * 2)
    scratch += buffers(slots, *[((tile, hid), bf16)] * 2)
    scratch += buffers(2, *[((rows, tile), t) for t in dtypes])

    def body(*refs):
        take = Refs(refs)
        (where,) = take(1)
        x_far, weights, out_far = take(2), take(2), take(count)

        def tile_at(n):
            return at(where[lax.div(n, share)] * share + lax.rem(n, share), tile)

        x = flows([lambda n, r=r: r for r in x_far], take(4))
        w = flows([lambda n, r=r: r.at[tile_at(n), :] for r in weights], take(4))
        o = flows([lambda n, r=r: r.at[:, at(n, tile)] for r in out_far], take(2 * count), True)
        for f in x:
            f.start(0)

        def compute(n, got, put):
            @pl.when(n == 0)
            def _():
                for f in x:
                    f.wait(0)

            put[0][...] = (
                contract_trailing_axis(x[0].close(0)[...], got[0][...])
                + contract_trailing_axis(x[1].close(0)[...], got[1][...])
            ).astype(put[0].dtype)

        tiles(count * share, w, *[([f], compute) for f in o])

    outs = [jax.ShapeDtypeStruct((rows, width), t) for t in dtypes]
    work = count * rows * width * hid
    estimate = cost(4 * work, 4 * work // rows)
    far = [*grads, in_hbm(gate), in_hbm(up)]
    return call(body, "input_parts", mark, [places], far, outs, scratch, 16, estimate)


def block_products(left, right):
    blocks, length, rank = left.shape
    width = right.shape[1]

    def body(l, r, out):
        out[0] = lax.dot_general(
            l[0], r[...], (((0,), (0,)), ((), ())), preferred_element_type=f32
        ).astype(bf16)

    return pl.pallas_call(
        body,
        grid=(blocks,),
        in_specs=[
            pl.BlockSpec((1, length, rank), lambda b: (b, 0, 0)),
            pl.BlockSpec((length, width), lambda b: (b, 0)),
        ],
        out_specs=pl.BlockSpec((1, rank, width), lambda b: (b, 0, 0)),
        out_shape=jax.ShapeDtypeStruct((blocks, rank, width), bf16),
        compiler_params=pltpu.CompilerParams(vmem_limit_bytes=16 << 20),
        cost_estimate=cost(2 * blocks * length * rank * width, left.size * 2 + right.size * 2),
        name="block_products",
    )(left, right)


def by_tenant(labels, scales, parts, tenants, at_once=4):
    count, rank, width = parts.shape

    def body(labels_ref, scales_ref, parts_ref, out):
        first = pl.program_id(0) * at_once
        out[...] = jnp.zeros_like(out)
        for c in range(count):
            offset = labels_ref[c] - first

            @pl.when((offset >= 0) & (offset < at_once))
            def _():
                out[offset] += scales_ref[c] * parts_ref[c].astype(f32)

    return pl.pallas_call(
        body,
        grid=(tenants // at_once,),
        in_specs=[SCALARS, SCALARS, pl.BlockSpec((count, rank, width), lambda t: (0, 0, 0))],
        out_specs=pl.BlockSpec((at_once, rank, width), lambda t: (t, 0, 0)),
        out_shape=jax.ShapeDtypeStruct((tenants, rank, width), f32),
        compiler_params=pltpu.CompilerParams(vmem_limit_bytes=16 << 20),
        cost_estimate=cost(0, 4 * tenants * rank * width),
        name="by_tenant",
    )(labels, scales, parts)


def ringed(
    tokens,
    cotangent,
    gate_weight,
    up_weight,
    down_matrix_frozen,
    adapter_a,
    adapter_b,
    tenant,
    ranks,
):
    rows, depth = tokens.shape
    blocks = tenant.shape[0]
    length = rows // blocks
    tenants, _, rank = adapter_a.shape
    devices = RING * PAIR
    me = lax.axis_index("tensor")
    along, across = me // PAIR, me % PAIR
    first_core = lax.axis_index("dp") == 0

    def place(k, j):
        return ((along + RING - k) % RING) * PAIR + (across + j) % PAIR

    def places(names):
        return jnp.stack([place(int(n[1]), int(n[2])) for n in names]).astype(jnp.int32)

    def ring_on(value):
        return lax.ppermute(value, "tensor", [(i, (i + PAIR) % devices) for i in range(devices)])

    def swap(value, bit=1):
        return lax.ppermute(value, "tensor", [(i, i ^ bit) for i in range(devices)])

    def other_core(value):
        return lax.ppermute(value, "dp", [(0, 1), (1, 0)])

    def both_cores(own, other):
        return jnp.where(
            first_core, jnp.concatenate([own, other]), jnp.concatenate([other, own])
        )

    adapter = adapter_a.transpose(0, 2, 1)
    ranks_of = ranks[tenant]
    mask = (lax.broadcasted_iota(jnp.int32, (blocks, 1, rank), 2) < ranks_of[:, None, None]).astype(f32)
    scales = adapter_alpha_factor / ranks.astype(f32)
    scale_of = scales[tenant]

    cot_blocks = cotangent.reshape(blocks, length, depth)
    back = jnp.einsum("bnd,brd->bnr", cot_blocks, adapter_b[tenant], preferred_element_type=f32)
    back = (back * mask).astype(bf16).reshape(rows * rank // depth, depth)

    held = {"T00": tokens, "C00": jnp.concatenate([cotangent, back])}
    slots = []
    mark = jnp.zeros(MARK.shape, MARK.dtype)

    def passed(*values):
        nonlocal mark
        *values, mark = together((*values, mark))
        return values

    def start(i):
        sent = []
        for plan, send, side in ((RING_PLAN, ring_on, 0), (PAIR_PLAN, swap, 1)):
            name, source = plan[i]
            value = held[source]
            if i >= 2:
                gate = slots[i - 2][side]
                if gate == source:
                    (value,) = passed(value)
                else:
                    value, held[gate] = passed(value, held[gate])
            held[name] = send(value)
            sent.append(name)
        slots.append(sent)

    def landed(i):
        names = slots[i]
        for n, v in zip(names, passed(*[held[n] for n in names])):
            held[n] = v

    def add_up(names, sums, low=None):
        nonlocal mark
        chunks = [held[n] for n in names]
        *out, mark = gate_up(mark, chunks, places(names), gate_weight, up_weight, sums, low)
        return out

    def add_down(names, total, last=None):
        nonlocal mark
        chunks = [held[n] for n in names]
        *out, mark = down_back(mark, chunks, rows, places(names), down_matrix_frozen, total, last)
        return out

    start(0)
    start(1)
    landed(0)
    labels = both_cores(tenant, other_core(tenant))
    label_scales = scales[labels]
    start(2)
    sums = add_up(["T00", "T10", "T01"], None)
    landed(1)
    start(3)
    (total,) = add_down(["C00", "C10", "C01"], None)
    landed(2)
    start(4)
    sums = add_up(["T20", "T11"], sums)
    landed(3)
    start(5)
    (total,) = add_down(["C20", "C11"], total)
    landed(4)
    start(6)
    sums = add_up(["T30", "T21"], sums)
    landed(5)
    act, slope, hidden, low = add_up(["T31"], sums, (tenant, adapter))
    low = low * mask
    got_low = swap(low)
    landed(6)
    back = sum(held[f"C{k}{j}"][rows:].astype(f32) for k in range(RING) for j in range(PAIR))
    back = back.reshape(blocks, length, rank)
    back = (back * scale_of[:, None, None]).astype(bf16)
    low, got_low = passed(low, got_low)
    low = low + got_low
    got_low = swap(low, PAIR)
    grads = add_down(["C30", "C21", "C31"], total, (tenant, adapter, back, act, slope))

    def parts(blocks_of, dtypes):
        nonlocal mark
        where = jnp.stack([place(k, j) for k, j in blocks_of]).astype(jnp.int32)
        *out, mark = input_parts(mark, where, grads, gate_weight, up_weight, depth, dtypes)
        return out

    def add(*terms):
        return sum(t.astype(f32) for t in terms).astype(bf16)

    (out0,) = parts([(1, 1)], [bf16])
    low, got_low = passed(low, got_low)
    low = low + got_low
    got_low = swap(low, 2 * PAIR)
    got0 = swap(out0)
    own0, out1 = parts([(1, 0), (2, 1)], [f32, bf16])
    got1 = swap(out1)
    got0, got_low = passed(got0, got_low)
    ring0 = ring_on(add(got0, own0))
    hidden, back = passed(hidden, back)
    block_a = block_products(back, hidden)
    other_a = other_core(block_a)
    (block_a,) = passed(block_a)
    own1, out2 = parts([(2, 0), (3, 1)], [f32, bf16])
    got2 = swap(out2)
    ring0, got1 = passed(ring0, got1)
    ring1 = ring_on(add(ring0, got1, own1))
    own2, out3 = parts([(3, 0), (0, 1)], [f32, bf16])
    got3 = swap(out3)
    ring1, got2 = passed(ring1, got2)
    ring2 = ring_on(add(ring1, got2, own2))
    (own3,) = parts([(0, 0)], [f32])

    low = (low + got_low).astype(bf16)
    low, block_a, other_a = passed(low, block_a, other_a)
    block_b = block_products(low, cotangent)
    other_b = other_core(block_b)
    ones = jnp.ones_like(label_scales)
    grad_a = by_tenant(labels, ones, both_cores(block_a, other_a), tenants)
    grad_b = by_tenant(labels, label_scales, both_cores(block_b, other_b), tenants)
    return add(ring2, got3, own3), grad_a.transpose(0, 2, 1), grad_b


def gathered(
    tokens,
    cotangent,
    gate_weight,
    up_weight,
    down_matrix_frozen,
    adapter_a,
    adapter_b,
    tenant,
    ranks,
):
    row_number_total = tokens.shape[0]
    block_count = tenant.shape[0]
    block_len = row_number_total // block_count
    rank_width = adapter_a.shape[2]
    tenant_count = adapter_a.shape[0]
    hidden_shard_slice = gate_weight.shape[1]
    shard_piece = lax.all_gather(tokens, "tensor", axis=1, tiled=True)
    gate_pre = jnp.dot(shard_piece, gate_weight, preferred_element_type=jnp.float32)
    up_pre = jnp.dot(shard_piece, up_weight, preferred_element_type=jnp.float32)
    sigma_gate = jax.nn.sigmoid(gate_pre)
    activated = gate_pre * sigma_gate
    hidden = (activated * up_pre).astype(jnp.bfloat16)
    mask_table = (
        lax.broadcasted_iota(jnp.int32, (tenant_count, rank_width), 1) < ranks[:, None]
    ).astype(jnp.float32)
    tenant_scale_lookup = adapter_alpha_factor / ranks.astype(jnp.float32)
    onehot = (
        tenant[:, None] == lax.broadcasted_iota(jnp.int32, (block_count, tenant_count), 1)
    ).astype(jnp.float32)
    block_mask = jnp.dot(onehot, mask_table, precision=lax.Precision.HIGHEST)
    block_scale = jnp.dot(onehot, tenant_scale_lookup, precision=lax.Precision.HIGHEST)
    hid_blocks = hidden.reshape(block_count, block_len, hidden_shard_slice)
    cot_blocks = cotangent.reshape(block_count, block_len, cotangent.shape[1])
    selected_down_adapter = adapter_a[tenant]
    b_chosen = adapter_b[tenant]
    low_part = jnp.einsum(
        "bnf,bfr->bnr", hid_blocks, selected_down_adapter, preferred_element_type=jnp.float32
    )
    back_part = jnp.einsum("bnd,brd->bnr", cot_blocks, b_chosen, preferred_element_type=jnp.float32)
    low_part = low_part * block_mask[:, None, :]
    back_part = back_part * block_mask[:, None, :]
    low_sum, back_sum = lax.psum((low_part, back_part), "tensor")
    low_bf = low_sum.astype(jnp.bfloat16)
    backward_half_precision = (back_sum * block_scale[:, None, None]).astype(jnp.bfloat16)
    adapter_gradient_term = jnp.einsum(
        "gpl,gdl->gpd",
        backward_half_precision,
        selected_down_adapter,
        preferred_element_type=jnp.float32,
    )
    adapter_gradient_term = adapter_gradient_term.reshape(row_number_total, hidden_shard_slice)
    hidden_gradient = adapter_gradient_term + contract_trailing_axis(
        lax.all_gather(cotangent, "tensor", axis=1, tiled=True), down_matrix_frozen
    )
    block_a = jnp.einsum(
        "bnf,bnr->bfr", hid_blocks, backward_half_precision, preferred_element_type=jnp.float32
    )
    grad_a_part = jnp.einsum("bt,bfr->tfr", onehot, block_a, precision=lax.Precision.HIGHEST)
    block_b = jnp.einsum("bnr,bnd->brd", low_bf, cot_blocks, preferred_element_type=jnp.float32)
    grad_b_part = jnp.einsum("bt,brd->trd", onehot, block_b, precision=lax.Precision.HIGHEST)
    grad_b_part = grad_b_part * tenant_scale_lookup[:, None, None]
    grad_a, grad_b = (
        lax.psum(grad_a_part.astype(jnp.bfloat16), "dp").astype(jnp.float32),
        lax.psum(grad_b_part.astype(jnp.bfloat16), "dp").astype(jnp.float32),
    )
    grad_gate = (
        hidden_gradient * up_pre * sigma_gate * (1.0 + gate_pre * (1.0 - sigma_gate))
    ).astype(jnp.bfloat16)
    grad_up = (hidden_gradient * activated).astype(jnp.bfloat16)
    input_term = contract_trailing_axis(grad_gate, gate_weight) + contract_trailing_axis(
        grad_up, up_weight
    )
    grad_input = lax.psum_scatter(input_term, "tensor", scatter_dimension=1, tiled=True).astype(
        jnp.bfloat16
    )
    return (grad_input, grad_a, grad_b)


def solution(mesh):
    sizes = mesh.shape
    local = ringed if (sizes["tensor"], sizes["dp"]) == (RING * PAIR, 2) else gathered
    return jax.shard_map(
        local,
        mesh=mesh,
        in_specs=(
            P(("groups", "dp"), "tensor"),
            P(("groups", "dp"), "tensor"),
            P(None, "tensor"),
            P(None, "tensor"),
            P("tensor", None),
            P("groups", "tensor", None),
            P("groups", None, "tensor"),
            P(("groups", "dp")),
            P("groups"),
        ),
        out_specs=(
            P(("groups", "dp"), "tensor"),
            P("groups", "tensor", None),
            P("groups", None, "tensor"),
        ),
        check_vma=False,
    )
```

```python
import functools

import jax
import jax.numpy as jnp
from jax import lax
from jax.experimental import pallas as pl
from jax.experimental.pallas import tpu as pltpu
from jax.sharding import PartitionSpec as P

adapter_alpha_factor = 32.0
f32 = jnp.float32
bf16 = jnp.bfloat16
together = lax.optimization_barrier

RING_PLAN = (
    ("T10", "T00"),
    ("C10", "C00"),
    ("T20", "T10"),
    ("C20", "C10"),
    ("T30", "T20"),
    ("C30", "C20"),
    ("C21", "C11"),
)
PAIR_PLAN = (
    ("T01", "T00"),
    ("C01", "C00"),
    ("T11", "T10"),
    ("C11", "C10"),
    ("T21", "T20"),
    ("T31", "T30"),
    ("C31", "C30"),
)
RING, PAIR = 4, 2


def contract_trailing_axis(left, right):
    return lax.dot_general(
        left, right, (((1,), (1,)), ((), ())), preferred_element_type=f32
    )


ANYWHERE = pl.BlockSpec(memory_space=pl.ANY)
NEAR = pl.BlockSpec(memory_space=pltpu.VMEM)
SCALARS = pl.BlockSpec(memory_space=pltpu.SMEM)
MARK = jax.ShapeDtypeStruct((8, 128), f32)


def cost(flops, weights):
    return pl.CostEstimate(flops=flops, bytes_accessed=weights, transcendentals=0)


def in_hbm(value):
    return pltpu.with_memory_space_constraint(value, pltpu.HBM)


def call(body, name, mark, scalars, far, out_shape, scratch, vmem, estimate):
    def marked(*refs):
        refs, (mark_ref, *scratch_refs) = refs[1 : ends + 1], refs[ends + 1 :]
        mark_ref[...] = jnp.zeros_like(mark_ref)
        body(*refs, *scratch_refs)

    ends = len(scalars) + len(far) + len(out_shape)
    return pl.pallas_call(
        marked,
        in_specs=[ANYWHERE] + [SCALARS] * len(scalars) + [ANYWHERE] * len(far),
        out_specs=[ANYWHERE] * len(out_shape) + [NEAR],
        out_shape=[*out_shape, MARK],
        scratch_shapes=scratch,
        compiler_params=pltpu.CompilerParams(vmem_limit_bytes=vmem << 20),
        cost_estimate=estimate,
        name=name,
    )(mark, *scalars, *far)


def at(index, size):
    return pl.ds(pl.multiple_of(index * size, size), size)


class Flow:
    def __init__(self, far, close, sems, out=False):
        self.far, self.close, self.sems, self.out = far, close, sems, out
        self.slots = sems.shape[0]

    def copy(self, n):
        ends = (self.close(n), self.far(n)) if self.out else (self.far(n), self.close(n))
        return pltpu.make_async_copy(*ends, self.sems.at[lax.rem(n, self.slots)])

    def start(self, n):
        self.copy(n).start()

    def wait(self, n):
        self.copy(n).wait()


def tiles(steps, whole, inward, *phases):
    for i in range(max(len(whole), len(inward))):
        for f in whole[i : i + 1] + inward[i : i + 1]:
            f.start(0)
    for n in range(1, steps):
        for f in inward:
            if n < f.slots:
                f.start(n)
    share = steps // len(phases)

    for p, (outward, compute) in enumerate(phases):

        def step(k, carry, base=p * share, outward=outward, compute=compute):
            n = base + k

            @pl.when(n == 0)
            def _():
                for f in whole:
                    f.wait(0)

            for f in inward:
                f.wait(n)
            for f in outward:

                @pl.when(k >= f.slots)
                def _():
                    f.wait(k - f.slots)

            compute(
                [f.close(0) for f in whole],
                [f.close(n) for f in inward],
                [f.close(k) for f in outward],
            )
            for f in outward:
                f.start(k)
            for f in inward:

                @pl.when(n + f.slots < steps)
                def _():
                    f.start(n + f.slots)

            return carry

        lax.fori_loop(0, share, step, 0)
    for outward, _ in phases:
        for f in outward:
            for k in range(max(0, share - f.slots), share):
                f.wait(k)


def buffers(slots, *shapes):
    out = []
    for shape, dtype in shapes:
        out += [pltpu.VMEM((slots, *shape), dtype), pltpu.SemaphoreType.DMA((slots,))]
    return out


def flows(fars, scratch, out=False):
    made = []
    for i, far in enumerate(fars):
        buffer, sems = scratch[2 * i : 2 * i + 2]
        made.append(Flow(far, lambda n, b=buffer: b.at[lax.rem(n, b.shape[0])], sems, out))
    return made


class Refs:
    def __init__(self, refs):
        self.refs = list(refs)

    def __call__(self, count):
        got, self.refs = self.refs[:count], self.refs[count:]
        return got


def gate_up(mark, chunks, places, gate, up, sums, low=None, tile=256, slots=3):
    count = len(chunks)
    rows, depth = chunks[0].shape
    hid = gate.shape[1]
    blocks = 0 if low is None else low[0].shape[0]
    length = 0 if low is None else rows // blocks
    rank = 0 if low is None else low[1].shape[1]
    scalars = [places] + ([] if low is None else [low[0]])
    far = [*chunks, gate, up] + ([] if sums is None else list(sums))
    far += [] if low is None else [low[1]]
    far = [in_hbm(f) for f in far]
    types = [f32, f32] if low is None else [f32, f32, bf16]
    outs = [pltpu.HBM((rows, hid), t) for t in types]
    if low is not None:
        outs += [jax.ShapeDtypeStruct((blocks, length, rank), f32)]
    scratch = buffers(1, *[((rows, depth), bf16)] * count)
    scratch += buffers(slots, *[((depth, tile), bf16)] * (2 * count))
    scratch += buffers(slots, *[((rows, tile), f32)] * (0 if sums is None else 2))
    scratch += buffers(2, *[((rank, tile), bf16)] * blocks)
    scratch += buffers(2, *[((rows, tile), t) for t in types])
    scratch += [] if low is None else buffers(1, ((blocks, length, rank), f32))

    def body(*refs):
        take = Refs(refs)
        (where,) = take(1)
        label = take(1)[0] if low is not None else None
        x_far = take(count)
        weights = take(2)
        sums_far = take(0 if sums is None else 2)
        adapter = take(0 if low is None else 1)
        out_far = take(len(types))
        low_far = take(0 if low is None else 1)
        x = flows([lambda n, r=r: r for r in x_far], take(2 * count))
        w = flows(
            [
                lambda n, r=r, c=c: r.at[at(where[c], depth), at(n, tile)]
                for r in weights
                for c in range(count)
            ],
            take(4 * count),
        )
        w += flows([lambda n, r=r: r.at[:, at(n, tile)] for r in sums_far], take(2 * len(sums_far)))
        w += flows(
            [lambda n, b=b: adapter[0].at[label[b], :, at(n, tile)] for b in range(blocks)],
            take(2 * blocks),
        )
        o = flows([lambda n, r=r: r.at[:, at(n, tile)] for r in out_far], take(2 * len(out_far)), True)
        l = flows([lambda n, r=r: r for r in low_far], take(2 * len(low_far)), True)
        for f in l:
            f.close(0)[...] = jnp.zeros((blocks, length, rank), f32)

        def compute(x, got, put):
            found = []
            for which in range(2):
                total = None
                for c in range(count):
                    term = jnp.dot(
                        x[c][...], got[which * count + c][...], preferred_element_type=f32
                    )
                    total = term if total is None else total + term
                if sums is not None:
                    total = total + got[2 * count + which][...]
                found.append(total)
            if low is None:
                put[0][...], put[1][...] = found
                return
            gate_pre, up_pre = found
            sigma = jax.nn.sigmoid(gate_pre)
            act = gate_pre * sigma
            put[0][...] = act
            put[1][...] = up_pre * sigma * (1.0 + gate_pre * (1.0 - sigma))
            hidden = (act * up_pre).astype(bf16)
            put[2][...] = hidden
            for b in range(blocks):
                l[0].close(0)[b] += contract_trailing_axis(
                    hidden[b * length : (b + 1) * length], got[len(got) - blocks + b][...]
                )

        tiles(hid // tile, x, w, (o, compute))
        for f in l:
            f.start(0)
            f.wait(0)

    work = count * rows * depth * hid
    estimate = cost(4 * work, 4 * work // rows)
    return call(body, "gate_up", mark, scalars, far, outs, scratch, 32, estimate)


def down_back(mark, chunks, rows, places, down, total, last=None, tile=256, slots=4):
    count = len(chunks)
    depth = chunks[0].shape[1]
    hid = down.shape[0]
    blocks = 0 if last is None else last[0].shape[0]
    length = 0 if last is None else rows // blocks
    rank = 0 if last is None else last[1].shape[1]
    scalars = [places] + ([] if last is None else [last[0]])
    far = [*chunks, down] + ([] if total is None else [total])
    far += [] if last is None else list(last[1:])
    far = [in_hbm(f) for f in far]
    types = [f32] if last is None else [bf16, bf16]
    scratch = buffers(1, *[((rows, depth), bf16)] * count)
    scratch += buffers(slots, *[((tile, depth), bf16)] * count)
    scratch += [] if total is None else buffers(slots, ((rows, tile), f32))
    if last is not None:
        scratch += buffers(1, ((blocks, length, rank), bf16))
        scratch += buffers(slots, *[((rank, tile), bf16)] * blocks)
        scratch += buffers(slots, *[((rows, tile), f32)] * 2)
    scratch += buffers(2, *[((rows, tile), t) for t in types])

    def body(*refs):
        take = Refs(refs)
        (where,) = take(1)
        label = take(1)[0] if last is not None else None
        x_far = take(count)
        (weight,) = take(1)
        total_far = take(0 if total is None else 1)
        adapter, back_far = take(0 if last is None else 2) or (None, None)
        factors = take(0 if last is None else 2)
        out_far = take(len(types))
        x = flows([lambda n, r=r: r.at[0:rows] for r in x_far], take(2 * count))
        w = flows(
            [lambda n, c=c: weight.at[at(n, tile), at(where[c], depth)] for c in range(count)],
            take(2 * count),
        )
        w += flows([lambda n, r=r: r.at[:, at(n, tile)] for r in total_far], take(2 * len(total_far)))
        if last is not None:
            x += flows([lambda n: back_far], take(2))
        w += flows(
            [lambda n, b=b: adapter.at[label[b], :, at(n, tile)] for b in range(blocks)],
            take(2 * blocks),
        )
        w += flows([lambda n, r=r: r.at[:, at(n, tile)] for r in factors], take(2 * len(factors)))
        o = flows([lambda n, r=r: r.at[:, at(n, tile)] for r in out_far], take(2 * len(out_far)), True)
        def compute(x, got, put):
            value = None
            for c in range(count):
                term = contract_trailing_axis(x[c][...], got[c][...])
                value = term if value is None else value + term
            if total is not None:
                value = value + got[count][...]
            if last is None:
                put[0][...] = value
                return
            *adapters, act, slope = got[len(got) - blocks - 2 :]
            back = x[count]
            for b in range(blocks):
                span = slice(b * length, (b + 1) * length)
                grad = value[span] + jnp.dot(
                    back[b], adapters[b][...], preferred_element_type=f32
                )
                put[0][span] = (grad * slope[span]).astype(bf16)
                put[1][span] = (grad * act[span]).astype(bf16)

        tiles(hid // tile, x, w, (o, compute))

    if last is None:
        outs = [pltpu.HBM((rows, hid), f32)]
    else:
        outs = [jax.ShapeDtypeStruct((rows, hid), bf16)] * 2
    work = count * rows * depth * hid
    estimate = cost(2 * work, 2 * work // rows)
    return call(body, "down_back", mark, scalars, far, outs, scratch, 24, estimate)


def input_parts(mark, places, grads, gate, up, width, count, tile=256, slots=4):
    rows, hid = grads[0].shape
    share = width // tile
    scratch = buffers(1, *[((rows, hid), bf16)] * 2)
    scratch += buffers(slots, *[((tile, hid), bf16)] * 2)
    scratch += buffers(2, *[((rows, tile), bf16)] * count)

    def body(*refs):
        take = Refs(refs)
        (where,) = take(1)
        x_far, weights, out_far = take(2), take(2), take(count)

        def tile_at(n):
            return at(where[lax.div(n, share)] * share + lax.rem(n, share), tile)

        x = flows([lambda n, r=r: r for r in x_far], take(4))
        w = flows([lambda n, r=r: r.at[tile_at(n), :] for r in weights], take(4))
        o = flows([lambda n, r=r: r.at[:, at(n, tile)] for r in out_far], take(2 * count), True)
        def compute(x, got, put):
            put[0][...] = (
                contract_trailing_axis(x[0][...], got[0][...])
                + contract_trailing_axis(x[1][...], got[1][...])
            ).astype(bf16)

        tiles(count * share, x, w, *[([f], compute) for f in o])

    outs = [jax.ShapeDtypeStruct((rows, width), bf16)] * count
    work = count * rows * width * hid
    estimate = cost(4 * work, 4 * work // rows)
    far = [*grads, in_hbm(gate), in_hbm(up)]
    return call(body, "input_parts", mark, [places], far, outs, scratch, 16, estimate)


def block_products(left, right):
    blocks, length, rank = left.shape
    width = right.shape[1]

    def body(l, r, out):
        out[0] = lax.dot_general(
            l[0], r[...], (((0,), (0,)), ((), ())), preferred_element_type=f32
        ).astype(bf16)

    return pl.pallas_call(
        body,
        grid=(blocks,),
        in_specs=[
            pl.BlockSpec((1, length, rank), lambda b: (b, 0, 0)),
            pl.BlockSpec((length, width), lambda b: (b, 0)),
        ],
        out_specs=pl.BlockSpec((1, rank, width), lambda b: (b, 0, 0)),
        out_shape=jax.ShapeDtypeStruct((blocks, rank, width), bf16),
        compiler_params=pltpu.CompilerParams(vmem_limit_bytes=16 << 20),
        cost_estimate=cost(2 * blocks * length * rank * width, left.size * 2 + right.size * 2),
        name="block_products",
    )(left, right)


def by_tenant(labels, scales, parts, tenants, at_once=4):
    count, rank, width = parts.shape

    def body(labels_ref, scales_ref, parts_ref, out):
        first = pl.program_id(0) * at_once
        out[...] = jnp.zeros_like(out)
        for c in range(count):
            offset = labels_ref[c] - first

            @pl.when((offset >= 0) & (offset < at_once))
            def _():
                out[offset] += scales_ref[c] * parts_ref[c].astype(f32)

    return pl.pallas_call(
        body,
        grid=(tenants // at_once,),
        in_specs=[SCALARS, SCALARS, pl.BlockSpec((count, rank, width), lambda t: (0, 0, 0))],
        out_specs=pl.BlockSpec((at_once, rank, width), lambda t: (t, 0, 0)),
        out_shape=jax.ShapeDtypeStruct((tenants, rank, width), f32),
        compiler_params=pltpu.CompilerParams(vmem_limit_bytes=16 << 20),
        cost_estimate=cost(0, 4 * tenants * rank * width),
        name="by_tenant",
    )(labels, scales, parts)


def ringed(
    tokens,
    cotangent,
    gate_weight,
    up_weight,
    down_matrix_frozen,
    adapter_a,
    adapter_b,
    tenant,
    ranks,
):
    rows, depth = tokens.shape
    blocks = tenant.shape[0]
    length = rows // blocks
    tenants, _, rank = adapter_a.shape
    devices = RING * PAIR
    me = lax.axis_index("tensor")
    along, across = me // PAIR, me % PAIR
    first_core = lax.axis_index("dp") == 0

    def place(k, j):
        return ((along + RING - k) % RING) * PAIR + (across + j) % PAIR

    def places(names):
        return jnp.stack([place(int(n[1]), int(n[2])) for n in names]).astype(jnp.int32)

    def ring_on(value):
        return lax.ppermute(value, "tensor", [(i, (i + PAIR) % devices) for i in range(devices)])

    def swap(value, bit=1):
        return lax.ppermute(value, "tensor", [(i, i ^ bit) for i in range(devices)])

    def other_core(value):
        return lax.ppermute(value, "dp", [(0, 1), (1, 0)])

    def both_cores(own, other):
        return jnp.where(
            first_core, jnp.concatenate([own, other]), jnp.concatenate([other, own])
        )

    adapter = adapter_a.transpose(0, 2, 1)
    ranks_of = ranks[tenant]
    mask_of = (lax.broadcasted_iota(jnp.int32, (blocks, 1, rank), 2) < ranks_of[:, None, None]).astype(f32)
    scales = adapter_alpha_factor / ranks.astype(f32)
    scale_of = scales[tenant]

    cot_blocks = cotangent.reshape(blocks, length, depth)
    back = jnp.einsum("bnd,brd->bnr", cot_blocks, adapter_b[tenant], preferred_element_type=f32)
    back = (back * mask_of).astype(bf16).reshape(rows * rank // depth, depth)

    held = {"T00": tokens, "C00": jnp.concatenate([cotangent, back])}
    mark = jnp.zeros(MARK.shape, MARK.dtype)

    def passed(*values):
        nonlocal mark
        *values, mark = together((*values, mark))
        return values

    def start(i, *sides):
        for side in sides or (0, 1):
            name, source = (RING_PLAN, PAIR_PLAN)[side][i]
            value = held[source]
            if i >= 2:
                gate = (RING_PLAN, PAIR_PLAN)[side][i - 2][0]
                if gate == source:
                    (value,) = passed(value)
                else:
                    value, held[gate] = passed(value, held[gate])
            held[name] = (ring_on, swap)[side](value)

    def landed(i):
        names = (RING_PLAN[i][0], PAIR_PLAN[i][0])
        for n, v in zip(names, passed(*[held[n] for n in names])):
            held[n] = v

    def add_up(names, sums, low=None):
        nonlocal mark
        chunks = [held[n] for n in names]
        *out, mark = gate_up(mark, chunks, places(names), gate_weight, up_weight, sums, low)
        return out

    def add_down(names, total, last=None):
        nonlocal mark
        chunks = [held[n] for n in names]
        *out, mark = down_back(mark, chunks, rows, places(names), down_matrix_frozen, total, last)
        return out

    start(0)
    start(1)
    landed(0)
    labels = both_cores(tenant, other_core(tenant))
    label_scales = scales[labels]
    start(2)
    sums = add_up(["T00", "T10", "T01"], None)
    landed(1)
    start(3)
    (total,) = add_down(["C00", "C10", "C01"], None)
    landed(2)
    start(4)
    sums = add_up(["T20", "T11"], sums)
    landed(3)
    start(5, 0)
    (total,) = add_down(["C20", "C11"], total)
    landed(4)
    start(5, 1)
    start(6, 0)
    sums = add_up(["T30", "T21"], sums)
    landed(5)
    start(6, 1)
    act, slope, hidden, low = add_up(["T31"], sums, (tenant, adapter))
    low = low * mask_of
    got_low = swap(low, PAIR)
    landed(6)
    back = sum(held[f"C{k}{j}"][rows:].astype(f32) for k in range(RING) for j in range(PAIR))
    back = back * jnp.repeat(scale_of, length * rank // depth)[:, None]
    back = back.astype(bf16).reshape(blocks, length, rank)
    grads = add_down(["C30", "C21", "C31"], total, (tenant, adapter, back, act, slope))

    def parts(*blocks_of):
        nonlocal mark
        where = jnp.stack([place(k, j) for k, j in blocks_of]).astype(jnp.int32)
        count = len(blocks_of)
        *out, mark = input_parts(mark, where, grads, gate_weight, up_weight, depth, count)
        return out

    def add(*terms):
        return sum(t.astype(f32) for t in terms).astype(bf16)

    low, got_low = passed(low, got_low)
    low = low + got_low
    (out0,) = parts((1, 1))
    got0 = swap(out0)
    (low,) = passed(low)
    got_low = swap(low, 2 * PAIR)
    own0, out1 = parts((1, 0), (2, 1))
    low, got_low = passed(low, got_low)
    low = low + got_low
    got_low = swap(low)
    got1 = swap(out1)
    (got0,) = passed(got0)
    ring0 = ring_on(add(got0, own0))
    own1, out2 = parts((2, 0), (3, 1))
    got2 = swap(out2)
    ring0, got1 = passed(ring0, got1)
    ring1 = ring_on(add(ring0, got1, own1))
    hidden, back = passed(hidden, back)
    block_a = block_products(back, hidden)
    other_a = other_core(block_a)
    (block_a,) = passed(block_a)
    own2, out3 = parts((3, 0), (0, 1))
    got3 = swap(out3)
    ring1, got2 = passed(ring1, got2)
    ring2 = ring_on(add(ring1, got2, own2))
    (own3,) = parts((0, 0))

    low = (low + got_low).astype(bf16)
    low, block_a, other_a = passed(low, block_a, other_a)
    block_b = block_products(low, cotangent)
    other_b = other_core(block_b)
    ones = jnp.ones_like(label_scales)
    grad_a = by_tenant(labels, ones, both_cores(block_a, other_a), tenants)
    grad_b = by_tenant(labels, label_scales, both_cores(block_b, other_b), tenants)
    return add(ring2, got3, own3), grad_a.transpose(0, 2, 1), grad_b


def gathered(
    tokens,
    cotangent,
    gate_weight,
    up_weight,
    down_matrix_frozen,
    adapter_a,
    adapter_b,
    tenant,
    ranks,
):
    row_number_total = tokens.shape[0]
    block_count = tenant.shape[0]
    block_len = row_number_total // block_count
    rank_width = adapter_a.shape[2]
    tenant_count = adapter_a.shape[0]
    hidden_shard_slice = gate_weight.shape[1]
    shard_piece = lax.all_gather(tokens, "tensor", axis=1, tiled=True)
    gate_pre = jnp.dot(shard_piece, gate_weight, preferred_element_type=jnp.float32)
    up_pre = jnp.dot(shard_piece, up_weight, preferred_element_type=jnp.float32)
    sigma_gate = jax.nn.sigmoid(gate_pre)
    activated = gate_pre * sigma_gate
    hidden = (activated * up_pre).astype(jnp.bfloat16)
    mask_table = (
        lax.broadcasted_iota(jnp.int32, (tenant_count, rank_width), 1) < ranks[:, None]
    ).astype(jnp.float32)
    tenant_scale_lookup = adapter_alpha_factor / ranks.astype(jnp.float32)
    onehot = (
        tenant[:, None] == lax.broadcasted_iota(jnp.int32, (block_count, tenant_count), 1)
    ).astype(jnp.float32)
    block_mask = jnp.dot(onehot, mask_table, precision=lax.Precision.HIGHEST)
    block_scale = jnp.dot(onehot, tenant_scale_lookup, precision=lax.Precision.HIGHEST)
    hid_blocks = hidden.reshape(block_count, block_len, hidden_shard_slice)
    cot_blocks = cotangent.reshape(block_count, block_len, cotangent.shape[1])
    selected_down_adapter = adapter_a[tenant]
    b_chosen = adapter_b[tenant]
    low_part = jnp.einsum(
        "bnf,bfr->bnr", hid_blocks, selected_down_adapter, preferred_element_type=jnp.float32
    )
    back_part = jnp.einsum("bnd,brd->bnr", cot_blocks, b_chosen, preferred_element_type=jnp.float32)
    low_part = low_part * block_mask[:, None, :]
    back_part = back_part * block_mask[:, None, :]
    low_sum, back_sum = lax.psum((low_part, back_part), "tensor")
    low_bf = low_sum.astype(jnp.bfloat16)
    backward_half_precision = (back_sum * block_scale[:, None, None]).astype(jnp.bfloat16)
    adapter_gradient_term = jnp.einsum(
        "gpl,gdl->gpd",
        backward_half_precision,
        selected_down_adapter,
        preferred_element_type=jnp.float32,
    )
    adapter_gradient_term = adapter_gradient_term.reshape(row_number_total, hidden_shard_slice)
    hidden_gradient = adapter_gradient_term + contract_trailing_axis(
        lax.all_gather(cotangent, "tensor", axis=1, tiled=True), down_matrix_frozen
    )
    block_a = jnp.einsum(
        "bnf,bnr->bfr", hid_blocks, backward_half_precision, preferred_element_type=jnp.float32
    )
    grad_a_part = jnp.einsum("bt,bfr->tfr", onehot, block_a, precision=lax.Precision.HIGHEST)
    block_b = jnp.einsum("bnr,bnd->brd", low_bf, cot_blocks, preferred_element_type=jnp.float32)
    grad_b_part = jnp.einsum("bt,brd->trd", onehot, block_b, precision=lax.Precision.HIGHEST)
    grad_b_part = grad_b_part * tenant_scale_lookup[:, None, None]
    grad_a, grad_b = (
        lax.psum(grad_a_part.astype(jnp.bfloat16), "dp").astype(jnp.float32),
        lax.psum(grad_b_part.astype(jnp.bfloat16), "dp").astype(jnp.float32),
    )
    grad_gate = (
        hidden_gradient * up_pre * sigma_gate * (1.0 + gate_pre * (1.0 - sigma_gate))
    ).astype(jnp.bfloat16)
    grad_up = (hidden_gradient * activated).astype(jnp.bfloat16)
    input_term = contract_trailing_axis(grad_gate, gate_weight) + contract_trailing_axis(
        grad_up, up_weight
    )
    grad_input = lax.psum_scatter(input_term, "tensor", scatter_dimension=1, tiled=True).astype(
        jnp.bfloat16
    )
    return (grad_input, grad_a, grad_b)


def solution(mesh):
    sizes = mesh.shape
    local = ringed if (sizes["tensor"], sizes["dp"]) == (RING * PAIR, 2) else gathered
    return jax.shard_map(
        local,
        mesh=mesh,
        in_specs=(
            P(("groups", "dp"), "tensor"),
            P(("groups", "dp"), "tensor"),
            P(None, "tensor"),
            P(None, "tensor"),
            P("tensor", None),
            P("groups", "tensor", None),
            P("groups", None, "tensor"),
            P(("groups", "dp")),
            P("groups"),
        ),
        out_specs=(
            P(("groups", "dp"), "tensor"),
            P("groups", "tensor", None),
            P("groups", None, "tensor"),
        ),
        check_vma=False,
    )
```

```python
import functools

import jax
import jax.numpy as jnp
from jax import lax
from jax.experimental import pallas as pl
from jax.experimental.pallas import tpu as pltpu
from jax.sharding import PartitionSpec as P

adapter_alpha_factor = 32.0
f32 = jnp.float32
bf16 = jnp.bfloat16
together = lax.optimization_barrier

RING_PLAN = (
    ("T10", "T00"),
    ("C10", "C00"),
    ("T20", "T10"),
    ("C20", "C10"),
    ("T30", "T20"),
    ("C30", "C20"),
    ("C21", "C11"),
)
PAIR_PLAN = (
    ("T01", "T00"),
    ("C01", "C00"),
    ("T11", "T10"),
    ("C11", "C10"),
    ("T21", "T20"),
    ("T31", "T30"),
    ("C31", "C30"),
)
RING, PAIR = 4, 2


def contract_trailing_axis(left, right):
    return lax.dot_general(
        left, right, (((1,), (1,)), ((), ())), preferred_element_type=f32
    )


ANYWHERE = pl.BlockSpec(memory_space=pl.ANY)
NEAR = pl.BlockSpec(memory_space=pltpu.VMEM)
SCALARS = pl.BlockSpec(memory_space=pltpu.SMEM)
MARK = jax.ShapeDtypeStruct((8, 128), f32)


def cost(flops, weights):
    return pl.CostEstimate(flops=flops, bytes_accessed=weights, transcendentals=0)


def in_hbm(value):
    return pltpu.with_memory_space_constraint(value, pltpu.HBM)


def call(body, name, mark, scalars, far, out_shape, scratch, vmem, estimate):
    def marked(*refs):
        refs, (mark_ref, *scratch_refs) = refs[1 : ends + 1], refs[ends + 1 :]
        mark_ref[...] = jnp.zeros_like(mark_ref)
        body(*refs, *scratch_refs)

    ends = len(scalars) + len(far) + len(out_shape)
    return pl.pallas_call(
        marked,
        in_specs=[ANYWHERE] + [SCALARS] * len(scalars) + [ANYWHERE] * len(far),
        out_specs=[ANYWHERE] * len(out_shape) + [NEAR],
        out_shape=[*out_shape, MARK],
        scratch_shapes=scratch,
        compiler_params=pltpu.CompilerParams(vmem_limit_bytes=vmem << 20),
        cost_estimate=estimate,
        name=name,
    )(mark, *scalars, *far)


def at(index, size):
    return pl.ds(pl.multiple_of(index * size, size), size)


class Flow:
    def __init__(self, far, close, sems, out=False):
        self.far, self.close, self.sems, self.out = far, close, sems, out
        self.slots = sems.shape[0]

    def copy(self, n):
        ends = (self.close(n), self.far(n)) if self.out else (self.far(n), self.close(n))
        return pltpu.make_async_copy(*ends, self.sems.at[lax.rem(n, self.slots)])

    def start(self, n):
        self.copy(n).start()

    def wait(self, n):
        self.copy(n).wait()


def tiles(steps, whole, inward, *phases):
    for i in range(max(len(whole), len(inward))):
        for f in whole[i : i + 1] + inward[i : i + 1]:
            f.start(0)
    for n in range(1, steps):
        for f in inward:
            if n < f.slots:
                f.start(n)
    share = steps // len(phases)

    for p, (outward, compute) in enumerate(phases):

        def step(k, carry, base=p * share, outward=outward, compute=compute):
            n = base + k

            @pl.when(n == 0)
            def _():
                for f in whole:
                    f.wait(0)

            for f in inward:
                f.wait(n)
            for f in outward:

                @pl.when(k >= f.slots)
                def _():
                    f.wait(k - f.slots)

            compute(
                [f.close(0) for f in whole],
                [f.close(n) for f in inward],
                [f.close(k) for f in outward],
            )
            for f in outward:
                f.start(k)
            for f in inward:

                @pl.when(n + f.slots < steps)
                def _():
                    f.start(n + f.slots)

            return carry

        lax.fori_loop(0, share, step, 0)
    for outward, _ in phases:
        for f in outward:
            for k in range(max(0, share - f.slots), share):
                f.wait(k)


def buffers(slots, *shapes):
    out = []
    for shape, dtype in shapes:
        out += [pltpu.VMEM((slots, *shape), dtype), pltpu.SemaphoreType.DMA((slots,))]
    return out


def flows(fars, scratch, out=False):
    made = []
    for i, far in enumerate(fars):
        buffer, sems = scratch[2 * i : 2 * i + 2]
        made.append(Flow(far, lambda n, b=buffer: b.at[lax.rem(n, b.shape[0])], sems, out))
    return made


class Refs:
    def __init__(self, refs):
        self.refs = list(refs)

    def __call__(self, count):
        got, self.refs = self.refs[:count], self.refs[count:]
        return got


def gate_up(mark, chunks, places, gate, up, sums, low=None, tile=256, slots=3):
    count = len(chunks)
    rows, depth = chunks[0].shape
    hid = gate.shape[1]
    blocks = 0 if low is None else low[0].shape[0]
    length = 0 if low is None else rows // blocks
    rank = 0 if low is None else low[1].shape[1]
    scalars = [places] + ([] if low is None else [low[0]])
    far = [*chunks, gate, up] + ([] if sums is None else list(sums))
    far += [] if low is None else [low[1]]
    far = [in_hbm(f) for f in far]
    types = [f32, f32] if low is None else [f32, f32, bf16]
    outs = [pltpu.HBM((rows, hid), t) for t in types]
    if low is not None:
        outs += [jax.ShapeDtypeStruct((blocks, length, rank), f32)]
    scratch = buffers(1, *[((rows, depth), bf16)] * count)
    scratch += buffers(slots, *[((depth, tile), bf16)] * (2 * count))
    scratch += buffers(slots, *[((rows, tile), f32)] * (0 if sums is None else 2))
    scratch += buffers(slots, *[((rank, tile), bf16)] * blocks)
    scratch += buffers(2, *[((rows, tile), t) for t in types])
    scratch += [] if low is None else buffers(1, ((blocks, length, rank), f32))

    def body(*refs):
        take = Refs(refs)
        (where,) = take(1)
        label = take(1)[0] if low is not None else None
        x_far = take(count)
        weights = take(2)
        sums_far = take(0 if sums is None else 2)
        adapter = take(0 if low is None else 1)
        out_far = take(len(types))
        low_far = take(0 if low is None else 1)
        x = flows([lambda n, r=r: r for r in x_far], take(2 * count))
        w = flows(
            [
                lambda n, r=r, c=c: r.at[at(where[c], depth), at(n, tile)]
                for r in weights
                for c in range(count)
            ],
            take(4 * count),
        )
        w += flows([lambda n, r=r: r.at[:, at(n, tile)] for r in sums_far], take(2 * len(sums_far)))
        w += flows(
            [lambda n, b=b: adapter[0].at[label[b], :, at(n, tile)] for b in range(blocks)],
            take(2 * blocks),
        )
        o = flows([lambda n, r=r: r.at[:, at(n, tile)] for r in out_far], take(2 * len(out_far)), True)
        l = flows([lambda n, r=r: r for r in low_far], take(2 * len(low_far)), True)
        for f in l:
            f.close(0)[...] = jnp.zeros((blocks, length, rank), f32)

        def compute(x, got, put):
            found = []
            for which in range(2):
                total = None
                for c in range(count):
                    term = jnp.dot(
                        x[c][...], got[which * count + c][...], preferred_element_type=f32
                    )
                    total = term if total is None else total + term
                if sums is not None:
                    total = total + got[2 * count + which][...]
                found.append(total)
            if low is None:
                put[0][...], put[1][...] = found
                return
            gate_pre, up_pre = found
            sigma = jax.nn.sigmoid(gate_pre)
            act = gate_pre * sigma
            put[0][...] = act
            put[1][...] = up_pre * sigma * (1.0 + gate_pre * (1.0 - sigma))
            hidden = (act * up_pre).astype(bf16)
            put[2][...] = hidden
            for b in range(blocks):
                l[0].close(0)[b] += contract_trailing_axis(
                    hidden[b * length : (b + 1) * length], got[len(got) - blocks + b][...]
                )

        tiles(hid // tile, x, w, (o, compute))
        for f in l:
            f.start(0)
            f.wait(0)

    work = count * rows * depth * hid
    estimate = cost(4 * work, 4 * work // rows)
    return call(body, "gate_up", mark, scalars, far, outs, scratch, 32, estimate)


def down_back(mark, chunks, rows, places, down, total, last=None, tile=256, slots=4):
    count = len(chunks)
    depth = chunks[0].shape[1]
    hid = down.shape[0]
    blocks = 0 if last is None else last[0].shape[0]
    length = 0 if last is None else rows // blocks
    rank = 0 if last is None else last[1].shape[1]
    scalars = [places] + ([] if last is None else [last[0]])
    far = [*chunks, down] + ([] if total is None else [total])
    far += [] if last is None else list(last[1:])
    far = [in_hbm(f) for f in far]
    types = [f32] if last is None else [bf16, bf16]
    scratch = buffers(1, *[((rows, depth), bf16)] * count)
    scratch += buffers(slots, *[((tile, depth), bf16)] * count)
    scratch += [] if total is None else buffers(slots, ((rows, tile), f32))
    if last is not None:
        scratch += buffers(1, ((blocks, length, rank), bf16))
        scratch += buffers(slots, *[((rank, tile), bf16)] * blocks)
        scratch += buffers(slots, *[((rows, tile), f32)] * 2)
    scratch += buffers(2, *[((rows, tile), t) for t in types])

    def body(*refs):
        take = Refs(refs)
        (where,) = take(1)
        label = take(1)[0] if last is not None else None
        x_far = take(count)
        (weight,) = take(1)
        total_far = take(0 if total is None else 1)
        adapter, back_far = take(0 if last is None else 2) or (None, None)
        factors = take(0 if last is None else 2)
        out_far = take(len(types))
        x = flows([lambda n, r=r: r.at[0:rows] for r in x_far], take(2 * count))
        w = flows(
            [lambda n, c=c: weight.at[at(n, tile), at(where[c], depth)] for c in range(count)],
            take(2 * count),
        )
        w += flows([lambda n, r=r: r.at[:, at(n, tile)] for r in total_far], take(2 * len(total_far)))
        if last is not None:
            x += flows([lambda n: back_far], take(2))
        w += flows(
            [lambda n, b=b: adapter.at[label[b], :, at(n, tile)] for b in range(blocks)],
            take(2 * blocks),
        )
        w += flows([lambda n, r=r: r.at[:, at(n, tile)] for r in factors], take(2 * len(factors)))
        o = flows([lambda n, r=r: r.at[:, at(n, tile)] for r in out_far], take(2 * len(out_far)), True)
        def compute(x, got, put):
            value = None
            for c in range(count):
                term = contract_trailing_axis(x[c][...], got[c][...])
                value = term if value is None else value + term
            if total is not None:
                value = value + got[count][...]
            if last is None:
                put[0][...] = value
                return
            *adapters, act, slope = got[len(got) - blocks - 2 :]
            back = x[count]
            for b in range(blocks):
                span = slice(b * length, (b + 1) * length)
                grad = value[span] + jnp.dot(
                    back[b], adapters[b][...], preferred_element_type=f32
                )
                put[0][span] = (grad * slope[span]).astype(bf16)
                put[1][span] = (grad * act[span]).astype(bf16)

        tiles(hid // tile, x, w, (o, compute))

    if last is None:
        outs = [pltpu.HBM((rows, hid), f32)]
    else:
        outs = [jax.ShapeDtypeStruct((rows, hid), bf16)] * 2
    work = count * rows * depth * hid
    estimate = cost(2 * work, 2 * work // rows)
    return call(body, "down_back", mark, scalars, far, outs, scratch, 24, estimate)


def input_parts(mark, places, grads, gate, up, width, count, tile=256, slots=4):
    rows, hid = grads[0].shape
    share = width // tile
    scratch = buffers(1, *[((rows, hid), bf16)] * 2)
    scratch += buffers(slots, *[((tile, hid), bf16)] * 2)
    scratch += buffers(2, *[((rows, tile), bf16)] * count)

    def body(*refs):
        take = Refs(refs)
        (where,) = take(1)
        x_far, weights, out_far = take(2), take(2), take(count)

        def tile_at(n):
            return at(where[lax.div(n, share)] * share + lax.rem(n, share), tile)

        x = flows([lambda n, r=r: r for r in x_far], take(4))
        w = flows([lambda n, r=r: r.at[tile_at(n), :] for r in weights], take(4))
        o = flows([lambda n, r=r: r.at[:, at(n, tile)] for r in out_far], take(2 * count), True)
        def compute(x, got, put):
            put[0][...] = (
                contract_trailing_axis(x[0][...], got[0][...])
                + contract_trailing_axis(x[1][...], got[1][...])
            ).astype(bf16)

        tiles(count * share, x, w, *[([f], compute) for f in o])

    outs = [jax.ShapeDtypeStruct((rows, width), bf16)] * count
    work = count * rows * width * hid
    estimate = cost(4 * work, 4 * work // rows)
    far = [*grads, in_hbm(gate), in_hbm(up)]
    return call(body, "input_parts", mark, [places], far, outs, scratch, 16, estimate)


def block_products(mark, left, right):
    blocks, length, rank = left.shape
    width = right.shape[1]

    def body(_, l, r, out):
        out[0] = lax.dot_general(
            l[0], r[...], (((0,), (0,)), ((), ())), preferred_element_type=f32
        ).astype(bf16)

    return pl.pallas_call(
        body,
        grid=(blocks,),
        in_specs=[
            ANYWHERE,
            pl.BlockSpec((1, length, rank), lambda b: (b, 0, 0)),
            pl.BlockSpec((length, width), lambda b: (b, 0)),
        ],
        out_specs=pl.BlockSpec((1, rank, width), lambda b: (b, 0, 0)),
        out_shape=jax.ShapeDtypeStruct((blocks, rank, width), bf16),
        compiler_params=pltpu.CompilerParams(vmem_limit_bytes=16 << 20),
        cost_estimate=cost(2 * blocks * length * rank * width, left.size * 2 + right.size * 2),
        name="block_products",
    )(mark, left, right)


def by_tenant(mark, labels, scales, parts, tenants, at_once=4):
    count, rank, width = parts.shape

    def body(_, labels_ref, scales_ref, parts_ref, out):
        first = pl.program_id(0) * at_once
        out[...] = jnp.zeros_like(out)
        for c in range(count):
            offset = labels_ref[c] - first

            @pl.when((offset >= 0) & (offset < at_once))
            def _():
                out[offset] += scales_ref[c] * parts_ref[c].astype(f32)

    return pl.pallas_call(
        body,
        grid=(tenants // at_once,),
        in_specs=[ANYWHERE, SCALARS, SCALARS, pl.BlockSpec((count, rank, width), lambda t: (0, 0, 0))],
        out_specs=pl.BlockSpec((at_once, rank, width), lambda t: (t, 0, 0)),
        out_shape=jax.ShapeDtypeStruct((tenants, rank, width), f32),
        compiler_params=pltpu.CompilerParams(vmem_limit_bytes=16 << 20),
        cost_estimate=cost(0, 4 * tenants * rank * width),
        name="by_tenant",
    )(mark, labels, scales, parts)


def ringed(
    tokens,
    cotangent,
    gate_weight,
    up_weight,
    down_matrix_frozen,
    adapter_a,
    adapter_b,
    tenant,
    ranks,
):
    rows, depth = tokens.shape
    blocks = tenant.shape[0]
    length = rows // blocks
    tenants, _, rank = adapter_a.shape
    devices = RING * PAIR
    me = lax.axis_index("tensor")
    along, across = me // PAIR, me % PAIR
    first_core = lax.axis_index("dp") == 0

    def place(k, j):
        return ((along + RING - k) % RING) * PAIR + (across + j) % PAIR

    def places(names):
        return jnp.stack([place(int(n[1]), int(n[2])) for n in names]).astype(jnp.int32)

    def ring_on(value):
        return lax.ppermute(value, "tensor", [(i, (i + PAIR) % devices) for i in range(devices)])

    def swap(value, bit=1):
        return lax.ppermute(value, "tensor", [(i, i ^ bit) for i in range(devices)])

    def other_core(value):
        return lax.ppermute(value, "dp", [(0, 1), (1, 0)])

    def both_cores(own, other):
        return jnp.where(
            first_core, jnp.concatenate([own, other]), jnp.concatenate([other, own])
        )

    adapter = adapter_a.transpose(0, 2, 1)
    ranks_of = ranks[tenant]
    mask_of = (lax.broadcasted_iota(jnp.int32, (blocks, 1, rank), 2) < ranks_of[:, None, None]).astype(f32)
    scales = adapter_alpha_factor / ranks.astype(f32)
    scale_of = scales[tenant]

    cot_blocks = cotangent.reshape(blocks, length, depth)
    back = jnp.einsum("bnd,brd->bnr", cot_blocks, adapter_b[tenant], preferred_element_type=f32)
    back = (back * mask_of).astype(bf16).reshape(rows * rank // depth, depth)

    held = {"T00": tokens, "C00": jnp.concatenate([cotangent, back])}
    mark = jnp.zeros(MARK.shape, MARK.dtype)

    def passed(*values):
        nonlocal mark
        *values, mark = together((*values, mark))
        return values

    def start(i, *sides):
        for side in sides or (0, 1):
            name, source = (RING_PLAN, PAIR_PLAN)[side][i]
            value = held[source]
            if i >= 2:
                gate = (RING_PLAN, PAIR_PLAN)[side][i - 2][0]
                if gate == source:
                    (value,) = passed(value)
                else:
                    value, held[gate] = passed(value, held[gate])
            held[name] = (ring_on, swap)[side](value)

    def landed(i):
        names = (RING_PLAN[i][0], PAIR_PLAN[i][0])
        for n, v in zip(names, passed(*[held[n] for n in names])):
            held[n] = v

    def add_up(names, sums, low=None):
        nonlocal mark
        chunks = [held[n] for n in names]
        *out, mark = gate_up(mark, chunks, places(names), gate_weight, up_weight, sums, low)
        return out

    def add_down(names, total, last=None):
        nonlocal mark
        chunks = [held[n] for n in names]
        *out, mark = down_back(mark, chunks, rows, places(names), down_matrix_frozen, total, last)
        return out

    start(0)
    start(1)
    landed(0)
    labels = both_cores(tenant, other_core(tenant))
    label_scales = scales[labels]
    start(2)
    sums = add_up(["T00", "T10", "T01"], None)
    landed(1)
    start(3)
    (total,) = add_down(["C00", "C10", "C01"], None)
    landed(2)
    start(4)
    sums = add_up(["T20", "T11"], sums)
    landed(3)
    start(5, 0)
    (total,) = add_down(["C20", "C11"], total)
    landed(4)
    start(5, 1)
    start(6, 0)
    sums = add_up(["T30"], sums)
    landed(5)
    start(6, 1)
    act, slope, hidden, low = add_up(["T21", "T31"], sums, (tenant, adapter))
    low = low * mask_of
    got_low = swap(low, PAIR)
    landed(6)
    back = sum(held[f"C{k}{j}"][rows:].astype(f32) for k in range(RING) for j in range(PAIR))
    back = back * jnp.repeat(scale_of, length * rank // depth)[:, None]
    back = back.astype(bf16).reshape(blocks, length, rank)
    grads = add_down(["C30", "C21", "C31"], total, (tenant, adapter, back, act, slope))

    def parts(*blocks_of):
        nonlocal mark
        where = jnp.stack([place(k, j) for k, j in blocks_of]).astype(jnp.int32)
        count = len(blocks_of)
        *out, mark = input_parts(mark, where, grads, gate_weight, up_weight, depth, count)
        return out

    def add(*terms):
        return sum(t.astype(f32) for t in terms).astype(bf16)

    low, got_low = passed(low, got_low)
    low = low + got_low
    (out0,) = parts((1, 1))
    got0 = swap(out0)
    (low,) = passed(low)
    got_low = swap(low, 2 * PAIR)
    own0, out1 = parts((1, 0), (2, 1))
    low, got_low = passed(low, got_low)
    low = low + got_low
    got_low = swap(low)
    got1 = swap(out1)
    (got0,) = passed(got0)
    ring0 = ring_on(add(got0, own0))
    own1, out2 = parts((2, 0), (3, 1))
    got2 = swap(out2)
    ring0, got1, low, got_low = passed(ring0, got1, low, got_low)
    ring1 = ring_on(add(ring0, got1, own1))
    hidden, back = passed(hidden, back)
    block_a = block_products(mark, back, hidden)
    block_b = block_products(mark, (low + got_low).astype(bf16), cotangent)
    other_a, other_b = other_core(block_a), other_core(block_b)
    block_a, block_b = passed(block_a, block_b)
    own2, out3 = parts((3, 0), (0, 1))
    got3 = swap(out3)
    ring1, got2, other_a, other_b = passed(ring1, got2, other_a, other_b)
    ring2 = ring_on(add(ring1, got2, own2))
    (own3,) = parts((0, 0))

    ones = jnp.ones_like(label_scales)
    grad_a = by_tenant(mark, labels, ones, both_cores(block_a, other_a), tenants)
    grad_b = by_tenant(mark, labels, label_scales, both_cores(block_b, other_b), tenants)
    return add(ring2, got3, own3), grad_a.transpose(0, 2, 1), grad_b


def gathered(
    tokens,
    cotangent,
    gate_weight,
    up_weight,
    down_matrix_frozen,
    adapter_a,
    adapter_b,
    tenant,
    ranks,
):
    row_number_total = tokens.shape[0]
    block_count = tenant.shape[0]
    block_len = row_number_total // block_count
    rank_width = adapter_a.shape[2]
    tenant_count = adapter_a.shape[0]
    hidden_shard_slice = gate_weight.shape[1]
    shard_piece = lax.all_gather(tokens, "tensor", axis=1, tiled=True)
    gate_pre = jnp.dot(shard_piece, gate_weight, preferred_element_type=jnp.float32)
    up_pre = jnp.dot(shard_piece, up_weight, preferred_element_type=jnp.float32)
    sigma_gate = jax.nn.sigmoid(gate_pre)
    activated = gate_pre * sigma_gate
    hidden = (activated * up_pre).astype(jnp.bfloat16)
    mask_table = (
        lax.broadcasted_iota(jnp.int32, (tenant_count, rank_width), 1) < ranks[:, None]
    ).astype(jnp.float32)
    tenant_scale_lookup = adapter_alpha_factor / ranks.astype(jnp.float32)
    onehot = (
        tenant[:, None] == lax.broadcasted_iota(jnp.int32, (block_count, tenant_count), 1)
    ).astype(jnp.float32)
    block_mask = jnp.dot(onehot, mask_table, precision=lax.Precision.HIGHEST)
    block_scale = jnp.dot(onehot, tenant_scale_lookup, precision=lax.Precision.HIGHEST)
    hid_blocks = hidden.reshape(block_count, block_len, hidden_shard_slice)
    cot_blocks = cotangent.reshape(block_count, block_len, cotangent.shape[1])
    selected_down_adapter = adapter_a[tenant]
    b_chosen = adapter_b[tenant]
    low_part = jnp.einsum(
        "bnf,bfr->bnr", hid_blocks, selected_down_adapter, preferred_element_type=jnp.float32
    )
    back_part = jnp.einsum("bnd,brd->bnr", cot_blocks, b_chosen, preferred_element_type=jnp.float32)
    low_part = low_part * block_mask[:, None, :]
    back_part = back_part * block_mask[:, None, :]
    low_sum, back_sum = lax.psum((low_part, back_part), "tensor")
    low_bf = low_sum.astype(jnp.bfloat16)
    backward_half_precision = (back_sum * block_scale[:, None, None]).astype(jnp.bfloat16)
    adapter_gradient_term = jnp.einsum(
        "gpl,gdl->gpd",
        backward_half_precision,
        selected_down_adapter,
        preferred_element_type=jnp.float32,
    )
    adapter_gradient_term = adapter_gradient_term.reshape(row_number_total, hidden_shard_slice)
    hidden_gradient = adapter_gradient_term + contract_trailing_axis(
        lax.all_gather(cotangent, "tensor", axis=1, tiled=True), down_matrix_frozen
    )
    block_a = jnp.einsum(
        "bnf,bnr->bfr", hid_blocks, backward_half_precision, preferred_element_type=jnp.float32
    )
    grad_a_part = jnp.einsum("bt,bfr->tfr", onehot, block_a, precision=lax.Precision.HIGHEST)
    block_b = jnp.einsum("bnr,bnd->brd", low_bf, cot_blocks, preferred_element_type=jnp.float32)
    grad_b_part = jnp.einsum("bt,brd->trd", onehot, block_b, precision=lax.Precision.HIGHEST)
    grad_b_part = grad_b_part * tenant_scale_lookup[:, None, None]
    grad_a, grad_b = (
        lax.psum(grad_a_part.astype(jnp.bfloat16), "dp").astype(jnp.float32),
        lax.psum(grad_b_part.astype(jnp.bfloat16), "dp").astype(jnp.float32),
    )
    grad_gate = (
        hidden_gradient * up_pre * sigma_gate * (1.0 + gate_pre * (1.0 - sigma_gate))
    ).astype(jnp.bfloat16)
    grad_up = (hidden_gradient * activated).astype(jnp.bfloat16)
    input_term = contract_trailing_axis(grad_gate, gate_weight) + contract_trailing_axis(
        grad_up, up_weight
    )
    grad_input = lax.psum_scatter(input_term, "tensor", scatter_dimension=1, tiled=True).astype(
        jnp.bfloat16
    )
    return (grad_input, grad_a, grad_b)


def solution(mesh):
    sizes = mesh.shape
    local = ringed if (sizes["tensor"], sizes["dp"]) == (RING * PAIR, 2) else gathered
    return jax.shard_map(
        local,
        mesh=mesh,
        in_specs=(
            P(("groups", "dp"), "tensor"),
            P(("groups", "dp"), "tensor"),
            P(None, "tensor"),
            P(None, "tensor"),
            P("tensor", None),
            P("groups", "tensor", None),
            P("groups", None, "tensor"),
            P(("groups", "dp")),
            P("groups"),
        ),
        out_specs=(
            P(("groups", "dp"), "tensor"),
            P("groups", "tensor", None),
            P("groups", None, "tensor"),
        ),
        check_vma=False,
    )
```

```python
import functools

import jax
import jax.numpy as jnp
from jax import lax
from jax.experimental import pallas as pl
from jax.experimental.pallas import tpu as pltpu
from jax.sharding import PartitionSpec as P

adapter_alpha_factor = 32.0
f32 = jnp.float32
bf16 = jnp.bfloat16
together = lax.optimization_barrier

RING_PLAN = (
    ("T10", "T00"),
    ("C10", "C00"),
    ("T20", "T10"),
    ("C20", "C10"),
    ("T30", "T20"),
    ("C30", "C20"),
    ("C21", "C11"),
)
PAIR_PLAN = (
    ("T01", "T00"),
    ("C01", "C00"),
    ("T11", "T10"),
    ("C11", "C10"),
    ("T21", "T20"),
    ("T31", "T30"),
    ("C31", "C30"),
)
RING, PAIR = 4, 2


def contract_trailing_axis(left, right):
    return lax.dot_general(
        left, right, (((1,), (1,)), ((), ())), preferred_element_type=f32
    )


ANYWHERE = pl.BlockSpec(memory_space=pl.ANY)
NEAR = pl.BlockSpec(memory_space=pltpu.VMEM)
SCALARS = pl.BlockSpec(memory_space=pltpu.SMEM)
MARK = jax.ShapeDtypeStruct((8, 128), f32)


def cost(flops, weights):
    return pl.CostEstimate(flops=flops, bytes_accessed=weights, transcendentals=0)


def in_hbm(value):
    return pltpu.with_memory_space_constraint(value, pltpu.HBM)


def call(body, name, mark, scalars, far, out_shape, scratch, vmem, estimate):
    def marked(*refs):
        refs, (mark_ref, *scratch_refs) = refs[1 : ends + 1], refs[ends + 1 :]
        mark_ref[...] = jnp.zeros_like(mark_ref)
        body(*refs, *scratch_refs)

    ends = len(scalars) + len(far) + len(out_shape)
    return pl.pallas_call(
        marked,
        in_specs=[ANYWHERE] + [SCALARS] * len(scalars) + [ANYWHERE] * len(far),
        out_specs=[ANYWHERE] * len(out_shape) + [NEAR],
        out_shape=[*out_shape, MARK],
        scratch_shapes=scratch,
        compiler_params=pltpu.CompilerParams(vmem_limit_bytes=vmem << 20),
        cost_estimate=estimate,
        name=name,
    )(mark, *scalars, *far)


def at(index, size):
    return pl.ds(pl.multiple_of(index * size, size), size)


class Flow:
    def __init__(self, far, close, sems, out=False):
        self.far, self.close, self.sems, self.out = far, close, sems, out
        self.slots = sems.shape[0]

    def copy(self, n):
        ends = (self.close(n), self.far(n)) if self.out else (self.far(n), self.close(n))
        return pltpu.make_async_copy(*ends, self.sems.at[lax.rem(n, self.slots)])

    def start(self, n):
        self.copy(n).start()

    def wait(self, n):
        self.copy(n).wait()


def tiles(steps, whole, inward, *phases):
    for i in range(max(len(whole), len(inward))):
        for f in whole[i : i + 1] + inward[i : i + 1]:
            f.start(0)
    for n in range(1, steps):
        for f in inward:
            if n < f.slots:
                f.start(n)
    share = steps // len(phases)

    for p, (outward, compute) in enumerate(phases):

        def step(k, carry, base=p * share, outward=outward, compute=compute):
            n = base + k

            @pl.when(n == 0)
            def _():
                for f in whole:
                    f.wait(0)

            for f in inward:
                f.wait(n)
            for f in outward:

                @pl.when(k >= f.slots)
                def _():
                    f.wait(k - f.slots)

            compute(
                [f.close(0) for f in whole],
                [f.close(n) for f in inward],
                [f.close(k) for f in outward],
            )
            for f in outward:
                f.start(k)
            for f in inward:

                @pl.when(n + f.slots < steps)
                def _():
                    f.start(n + f.slots)

            return carry

        lax.fori_loop(0, share, step, 0)
    for outward, _ in phases:
        for f in outward:
            for k in range(max(0, share - f.slots), share):
                f.wait(k)


def buffers(slots, *shapes):
    out = []
    for shape, dtype in shapes:
        out += [pltpu.VMEM((slots, *shape), dtype), pltpu.SemaphoreType.DMA((slots,))]
    return out


def flows(fars, scratch, out=False):
    made = []
    for i, far in enumerate(fars):
        buffer, sems = scratch[2 * i : 2 * i + 2]
        made.append(Flow(far, lambda n, b=buffer: b.at[lax.rem(n, b.shape[0])], sems, out))
    return made


class Refs:
    def __init__(self, refs):
        self.refs = list(refs)

    def __call__(self, count):
        got, self.refs = self.refs[:count], self.refs[count:]
        return got


def gate_up(mark, chunks, places, gate, up, sums, low=None, tile=256, slots=3):
    count = len(chunks)
    rows, depth = chunks[0].shape
    hid = gate.shape[1]
    blocks = 0 if low is None else low[0].shape[0]
    length = 0 if low is None else rows // blocks
    rank = 0 if low is None else low[1].shape[1]
    scalars = [places] + ([] if low is None else [low[0]])
    far = [*chunks, gate, up] + ([] if sums is None else list(sums))
    far += [] if low is None else [low[1]]
    far = [in_hbm(f) for f in far]
    types = [f32, f32] if low is None else [f32, f32, bf16]
    outs = [pltpu.HBM((rows, hid), t) for t in types]
    if low is not None:
        outs += [jax.ShapeDtypeStruct((blocks, length, rank), f32)]
    scratch = buffers(1, *[((rows, depth), bf16)] * count)
    scratch += buffers(slots, *[((depth, tile), bf16)] * (2 * count))
    scratch += buffers(slots, *[((rows, tile), f32)] * (0 if sums is None else 2))
    scratch += buffers(slots, *[((rank, tile), bf16)] * blocks)
    scratch += buffers(2, *[((rows, tile), t) for t in types])
    scratch += [] if low is None else buffers(1, ((blocks, length, rank), f32))

    def body(*refs):
        take = Refs(refs)
        (where,) = take(1)
        label = take(1)[0] if low is not None else None
        x_far = take(count)
        weights = take(2)
        sums_far = take(0 if sums is None else 2)
        adapter = take(0 if low is None else 1)
        out_far = take(len(types))
        low_far = take(0 if low is None else 1)
        x = flows([lambda n, r=r: r for r in x_far], take(2 * count))
        w = flows(
            [
                lambda n, r=r, c=c: r.at[at(where[c], depth), at(n, tile)]
                for r in weights
                for c in range(count)
            ],
            take(4 * count),
        )
        w += flows([lambda n, r=r: r.at[:, at(n, tile)] for r in sums_far], take(2 * len(sums_far)))
        w += flows(
            [lambda n, b=b: adapter[0].at[label[b], :, at(n, tile)] for b in range(blocks)],
            take(2 * blocks),
        )
        o = flows([lambda n, r=r: r.at[:, at(n, tile)] for r in out_far], take(2 * len(out_far)), True)
        l = flows([lambda n, r=r: r for r in low_far], take(2 * len(low_far)), True)
        for f in l:
            f.close(0)[...] = jnp.zeros((blocks, length, rank), f32)

        def compute(x, got, put):
            found = []
            for which in range(2):
                total = None
                for c in range(count):
                    term = jnp.dot(
                        x[c][...], got[which * count + c][...], preferred_element_type=f32
                    )
                    total = term if total is None else total + term
                if sums is not None:
                    total = total + got[2 * count + which][...]
                found.append(total)
            if low is None:
                put[0][...], put[1][...] = found
                return
            gate_pre, up_pre = found
            sigma = jax.nn.sigmoid(gate_pre)
            act = gate_pre * sigma
            put[0][...] = act
            put[1][...] = up_pre * sigma * (1.0 + gate_pre * (1.0 - sigma))
            hidden = (act * up_pre).astype(bf16)
            put[2][...] = hidden
            for b in range(blocks):
                l[0].close(0)[b] += contract_trailing_axis(
                    hidden[b * length : (b + 1) * length], got[len(got) - blocks + b][...]
                )

        tiles(hid // tile, x, w, (o, compute))
        for f in l:
            f.start(0)
            f.wait(0)

    work = count * rows * depth * hid
    estimate = cost(4 * work, 4 * work // rows)
    return call(body, "gate_up", mark, scalars, far, outs, scratch, 32, estimate)


def down_back(mark, chunks, rows, places, down, total, last=None, tile=256, slots=4):
    count = len(chunks)
    depth = chunks[0].shape[1]
    hid = down.shape[0]
    blocks = 0 if last is None else last[0].shape[0]
    length = 0 if last is None else rows // blocks
    rank = 0 if last is None else last[1].shape[1]
    scalars = [places] + ([] if last is None else [last[0]])
    far = [*chunks, down] + ([] if total is None else [total])
    far += [] if last is None else list(last[1:])
    far = [in_hbm(f) for f in far]
    types = [f32] if last is None else [bf16, bf16]
    scratch = buffers(1, *[((rows, depth), bf16)] * count)
    scratch += buffers(slots, *[((tile, depth), bf16)] * count)
    scratch += [] if total is None else buffers(slots, ((rows, tile), f32))
    if last is not None:
        scratch += buffers(1, ((blocks, length, rank), bf16))
        scratch += buffers(slots, *[((rank, tile), bf16)] * blocks)
        scratch += buffers(slots, *[((rows, tile), f32)] * 2)
    scratch += buffers(2, *[((rows, tile), t) for t in types])

    def body(*refs):
        take = Refs(refs)
        (where,) = take(1)
        label = take(1)[0] if last is not None else None
        x_far = take(count)
        (weight,) = take(1)
        total_far = take(0 if total is None else 1)
        adapter, back_far = take(0 if last is None else 2) or (None, None)
        factors = take(0 if last is None else 2)
        out_far = take(len(types))
        x = flows([lambda n, r=r: r.at[0:rows] for r in x_far], take(2 * count))
        w = flows(
            [lambda n, c=c: weight.at[at(n, tile), at(where[c], depth)] for c in range(count)],
            take(2 * count),
        )
        w += flows([lambda n, r=r: r.at[:, at(n, tile)] for r in total_far], take(2 * len(total_far)))
        if last is not None:
            x += flows([lambda n: back_far], take(2))
        w += flows(
            [lambda n, b=b: adapter.at[label[b], :, at(n, tile)] for b in range(blocks)],
            take(2 * blocks),
        )
        w += flows([lambda n, r=r: r.at[:, at(n, tile)] for r in factors], take(2 * len(factors)))
        o = flows([lambda n, r=r: r.at[:, at(n, tile)] for r in out_far], take(2 * len(out_far)), True)
        def compute(x, got, put):
            value = None
            for c in range(count):
                term = contract_trailing_axis(x[c][...], got[c][...])
                value = term if value is None else value + term
            if total is not None:
                value = value + got[count][...]
            if last is None:
                put[0][...] = value
                return
            *adapters, act, slope = got[len(got) - blocks - 2 :]
            back = x[count]
            for b in range(blocks):
                span = slice(b * length, (b + 1) * length)
                grad = value[span] + jnp.dot(
                    back[b], adapters[b][...], preferred_element_type=f32
                )
                put[0][span] = (grad * slope[span]).astype(bf16)
                put[1][span] = (grad * act[span]).astype(bf16)

        tiles(hid // tile, x, w, (o, compute))

    if last is None:
        outs = [pltpu.HBM((rows, hid), f32)]
    else:
        outs = [jax.ShapeDtypeStruct((rows, hid), bf16)] * 2
    work = count * rows * depth * hid
    estimate = cost(2 * work, 2 * work // rows)
    return call(body, "down_back", mark, scalars, far, outs, scratch, 24, estimate)


def input_parts(mark, places, grads, gate, up, width, count, tile=256, slots=4):
    rows, hid = grads[0].shape
    share = width // tile
    scratch = buffers(1, *[((rows, hid), bf16)] * 2)
    scratch += buffers(slots, *[((tile, hid), bf16)] * 2)
    scratch += buffers(2, *[((rows, tile), bf16)] * count)

    def body(*refs):
        take = Refs(refs)
        (where,) = take(1)
        x_far, weights, out_far = take(2), take(2), take(count)

        def tile_at(n):
            return at(where[lax.div(n, share)] * share + lax.rem(n, share), tile)

        x = flows([lambda n, r=r: r for r in x_far], take(4))
        w = flows([lambda n, r=r: r.at[tile_at(n), :] for r in weights], take(4))
        o = flows([lambda n, r=r: r.at[:, at(n, tile)] for r in out_far], take(2 * count), True)
        def compute(x, got, put):
            put[0][...] = (
                contract_trailing_axis(x[0][...], got[0][...])
                + contract_trailing_axis(x[1][...], got[1][...])
            ).astype(bf16)

        tiles(count * share, x, w, *[([f], compute) for f in o])

    outs = [jax.ShapeDtypeStruct((rows, width), bf16)] * count
    work = count * rows * width * hid
    estimate = cost(4 * work, 4 * work // rows)
    far = [*grads, in_hbm(gate), in_hbm(up)]
    return call(body, "input_parts", mark, [places], far, outs, scratch, 16, estimate)


def block_products(mark, left, right):
    blocks, length, rank = left.shape
    width = right.shape[1]

    def body(_, l, r, out):
        out[0] = lax.dot_general(
            l[0], r[...], (((0,), (0,)), ((), ())), preferred_element_type=f32
        ).astype(bf16)

    return pl.pallas_call(
        body,
        grid=(blocks,),
        in_specs=[
            ANYWHERE,
            pl.BlockSpec((1, length, rank), lambda b: (b, 0, 0)),
            pl.BlockSpec((length, width), lambda b: (b, 0)),
        ],
        out_specs=pl.BlockSpec((1, rank, width), lambda b: (b, 0, 0)),
        out_shape=jax.ShapeDtypeStruct((blocks, rank, width), bf16),
        compiler_params=pltpu.CompilerParams(vmem_limit_bytes=16 << 20),
        cost_estimate=cost(2 * blocks * length * rank * width, left.size * 2 + right.size * 2),
        name="block_products",
    )(mark, left, right)


def by_tenant(mark, labels, scales, parts, tenants, at_once=4):
    count, rank, width = parts.shape

    def body(_, labels_ref, scales_ref, parts_ref, out):
        first = pl.program_id(0) * at_once
        out[...] = jnp.zeros_like(out)
        for c in range(count):
            offset = labels_ref[c] - first

            @pl.when((offset >= 0) & (offset < at_once))
            def _():
                out[offset] += scales_ref[c] * parts_ref[c].astype(f32)

    return pl.pallas_call(
        body,
        grid=(tenants // at_once,),
        in_specs=[ANYWHERE, SCALARS, SCALARS, pl.BlockSpec((count, rank, width), lambda t: (0, 0, 0))],
        out_specs=pl.BlockSpec((at_once, rank, width), lambda t: (t, 0, 0)),
        out_shape=jax.ShapeDtypeStruct((tenants, rank, width), f32),
        compiler_params=pltpu.CompilerParams(vmem_limit_bytes=16 << 20),
        cost_estimate=cost(0, 4 * tenants * rank * width),
        name="by_tenant",
    )(mark, labels, scales, parts)


def ringed(
    tokens,
    cotangent,
    gate_weight,
    up_weight,
    down_matrix_frozen,
    adapter_a,
    adapter_b,
    tenant,
    ranks,
):
    rows, depth = tokens.shape
    blocks = tenant.shape[0]
    length = rows // blocks
    tenants, _, rank = adapter_a.shape
    devices = RING * PAIR
    me = lax.axis_index("tensor")
    along, across = me // PAIR, me % PAIR
    first_core = lax.axis_index("dp") == 0

    def place(k, j):
        return ((along + RING - k) % RING) * PAIR + (across + j) % PAIR

    def places(names):
        return jnp.stack([place(int(n[1]), int(n[2])) for n in names]).astype(jnp.int32)

    def ring_on(value):
        return lax.ppermute(value, "tensor", [(i, (i + PAIR) % devices) for i in range(devices)])

    def swap(value, bit=1):
        return lax.ppermute(value, "tensor", [(i, i ^ bit) for i in range(devices)])

    def other_core(value):
        return lax.ppermute(value, "dp", [(0, 1), (1, 0)])

    def both_cores(own, other):
        return jnp.where(
            first_core, jnp.concatenate([own, other]), jnp.concatenate([other, own])
        )

    adapter = adapter_a.transpose(0, 2, 1)
    ranks_of = ranks[tenant]
    mask_of = (lax.broadcasted_iota(jnp.int32, (blocks, 1, rank), 2) < ranks_of[:, None, None]).astype(f32)
    scales = adapter_alpha_factor / ranks.astype(f32)
    scale_of = scales[tenant]

    cot_blocks = cotangent.reshape(blocks, length, depth)
    back = jnp.einsum("bnd,brd->bnr", cot_blocks, adapter_b[tenant], preferred_element_type=f32)
    back = (back * mask_of).astype(bf16).reshape(rows * rank // depth, depth)

    held = {"T00": tokens, "C00": jnp.concatenate([cotangent, back])}
    mark = jnp.zeros(MARK.shape, MARK.dtype)

    def passed(*values):
        nonlocal mark
        *values, mark = together((*values, mark))
        return values

    def start(i, *sides):
        for side in sides or (0, 1):
            name, source = (RING_PLAN, PAIR_PLAN)[side][i]
            value = held[source]
            if i >= 2:
                gate = (RING_PLAN, PAIR_PLAN)[side][i - 2][0]
                if gate == source:
                    (value,) = passed(value)
                else:
                    value, held[gate] = passed(value, held[gate])
            held[name] = (ring_on, swap)[side](value)

    def landed(i):
        names = (RING_PLAN[i][0], PAIR_PLAN[i][0])
        for n, v in zip(names, passed(*[held[n] for n in names])):
            held[n] = v

    def add_up(names, sums, low=None):
        nonlocal mark
        chunks = [held[n] for n in names]
        *out, mark = gate_up(mark, chunks, places(names), gate_weight, up_weight, sums, low)
        return out

    def add_down(names, total, last=None):
        nonlocal mark
        chunks = [held[n] for n in names]
        *out, mark = down_back(mark, chunks, rows, places(names), down_matrix_frozen, total, last)
        return out

    start(0)
    start(1)
    landed(0)
    labels = both_cores(tenant, other_core(tenant))
    label_scales = scales[labels]
    start(2)
    sums = add_up(["T00", "T10", "T01"], None)
    landed(1)
    start(3)
    (total,) = add_down(["C00", "C10", "C01"], None)
    landed(2)
    start(4)
    sums = add_up(["T20", "T11"], sums)
    landed(3)
    start(5, 0)
    (total,) = add_down(["C20", "C11"], total)
    landed(4)
    start(5, 1)
    start(6, 0)
    sums = add_up(["T30"], sums)
    landed(5)
    start(6, 1)
    act, slope, hidden, low = add_up(["T21", "T31"], sums, (tenant, adapter))
    low = low * mask_of
    got_low = swap(low, PAIR)
    landed(6)
    back = sum(held[f"C{k}{j}"][rows:].astype(f32) for k in range(RING) for j in range(PAIR))
    back = back * jnp.repeat(scale_of, length * rank // depth)[:, None]
    back = back.astype(bf16).reshape(blocks, length, rank)
    grads = add_down(["C30", "C21", "C31"], total, (tenant, adapter, back, act, slope))

    def parts(*blocks_of):
        nonlocal mark
        where = jnp.stack([place(k, j) for k, j in blocks_of]).astype(jnp.int32)
        count = len(blocks_of)
        *out, mark = input_parts(mark, where, grads, gate_weight, up_weight, depth, count)
        return out

    def add(*terms):
        return sum(t.astype(f32) for t in terms).astype(bf16)

    low, got_low = passed(low, got_low)
    low = low + got_low
    (out0,) = parts((1, 1))
    got0 = swap(out0)
    (low,) = passed(low)
    got_low = swap(low, 2 * PAIR)
    own0, out1 = parts((1, 0), (2, 1))
    low, got_low = passed(low, got_low)
    low = low + got_low
    got_low = swap(low.astype(bf16))
    got1 = swap(out1)
    (got0,) = passed(got0)
    ring0 = ring_on(add(got0, own0))
    own1, out2 = parts((2, 0), (3, 1))
    got2 = swap(out2)
    ring0, got1, low, got_low = passed(ring0, got1, low, got_low)
    ring1 = ring_on(add(ring0, got1, own1))
    hidden, back = passed(hidden, back)
    block_a = block_products(mark, back, hidden)
    block_b = block_products(mark, (low + got_low).astype(bf16), cotangent)
    other_a, other_b = other_core(block_a), other_core(block_b)
    block_a, block_b = passed(block_a, block_b)
    own2, out3 = parts((3, 0), (0, 1))
    got3 = swap(out3)
    ring1, got2, other_a, other_b = passed(ring1, got2, other_a, other_b)
    ring2 = ring_on(add(ring1, got2, own2))
    (own3,) = parts((0, 0))

    ones = jnp.ones_like(label_scales)
    grad_a = by_tenant(mark, labels, ones, both_cores(block_a, other_a), tenants)
    grad_b = by_tenant(mark, labels, label_scales, both_cores(block_b, other_b), tenants)
    return add(ring2, got3, own3), grad_a.transpose(0, 2, 1), grad_b


def gathered(
    tokens,
    cotangent,
    gate_weight,
    up_weight,
    down_matrix_frozen,
    adapter_a,
    adapter_b,
    tenant,
    ranks,
):
    row_number_total = tokens.shape[0]
    block_count = tenant.shape[0]
    block_len = row_number_total // block_count
    rank_width = adapter_a.shape[2]
    tenant_count = adapter_a.shape[0]
    hidden_shard_slice = gate_weight.shape[1]
    shard_piece = lax.all_gather(tokens, "tensor", axis=1, tiled=True)
    gate_pre = jnp.dot(shard_piece, gate_weight, preferred_element_type=jnp.float32)
    up_pre = jnp.dot(shard_piece, up_weight, preferred_element_type=jnp.float32)
    sigma_gate = jax.nn.sigmoid(gate_pre)
    activated = gate_pre * sigma_gate
    hidden = (activated * up_pre).astype(jnp.bfloat16)
    mask_table = (
        lax.broadcasted_iota(jnp.int32, (tenant_count, rank_width), 1) < ranks[:, None]
    ).astype(jnp.float32)
    tenant_scale_lookup = adapter_alpha_factor / ranks.astype(jnp.float32)
    onehot = (
        tenant[:, None] == lax.broadcasted_iota(jnp.int32, (block_count, tenant_count), 1)
    ).astype(jnp.float32)
    block_mask = jnp.dot(onehot, mask_table, precision=lax.Precision.HIGHEST)
    block_scale = jnp.dot(onehot, tenant_scale_lookup, precision=lax.Precision.HIGHEST)
    hid_blocks = hidden.reshape(block_count, block_len, hidden_shard_slice)
    cot_blocks = cotangent.reshape(block_count, block_len, cotangent.shape[1])
    selected_down_adapter = adapter_a[tenant]
    b_chosen = adapter_b[tenant]
    low_part = jnp.einsum(
        "bnf,bfr->bnr", hid_blocks, selected_down_adapter, preferred_element_type=jnp.float32
    )
    back_part = jnp.einsum("bnd,brd->bnr", cot_blocks, b_chosen, preferred_element_type=jnp.float32)
    low_part = low_part * block_mask[:, None, :]
    back_part = back_part * block_mask[:, None, :]
    low_sum, back_sum = lax.psum((low_part, back_part), "tensor")
    low_bf = low_sum.astype(jnp.bfloat16)
    backward_half_precision = (back_sum * block_scale[:, None, None]).astype(jnp.bfloat16)
    adapter_gradient_term = jnp.einsum(
        "gpl,gdl->gpd",
        backward_half_precision,
        selected_down_adapter,
        preferred_element_type=jnp.float32,
    )
    adapter_gradient_term = adapter_gradient_term.reshape(row_number_total, hidden_shard_slice)
    hidden_gradient = adapter_gradient_term + contract_trailing_axis(
        lax.all_gather(cotangent, "tensor", axis=1, tiled=True), down_matrix_frozen
    )
    block_a = jnp.einsum(
        "bnf,bnr->bfr", hid_blocks, backward_half_precision, preferred_element_type=jnp.float32
    )
    grad_a_part = jnp.einsum("bt,bfr->tfr", onehot, block_a, precision=lax.Precision.HIGHEST)
    block_b = jnp.einsum("bnr,bnd->brd", low_bf, cot_blocks, preferred_element_type=jnp.float32)
    grad_b_part = jnp.einsum("bt,brd->trd", onehot, block_b, precision=lax.Precision.HIGHEST)
    grad_b_part = grad_b_part * tenant_scale_lookup[:, None, None]
    grad_a, grad_b = (
        lax.psum(grad_a_part.astype(jnp.bfloat16), "dp").astype(jnp.float32),
        lax.psum(grad_b_part.astype(jnp.bfloat16), "dp").astype(jnp.float32),
    )
    grad_gate = (
        hidden_gradient * up_pre * sigma_gate * (1.0 + gate_pre * (1.0 - sigma_gate))
    ).astype(jnp.bfloat16)
    grad_up = (hidden_gradient * activated).astype(jnp.bfloat16)
    input_term = contract_trailing_axis(grad_gate, gate_weight) + contract_trailing_axis(
        grad_up, up_weight
    )
    grad_input = lax.psum_scatter(input_term, "tensor", scatter_dimension=1, tiled=True).astype(
        jnp.bfloat16
    )
    return (grad_input, grad_a, grad_b)


def solution(mesh):
    sizes = mesh.shape
    local = ringed if (sizes["tensor"], sizes["dp"]) == (RING * PAIR, 2) else gathered
    return jax.shard_map(
        local,
        mesh=mesh,
        in_specs=(
            P(("groups", "dp"), "tensor"),
            P(("groups", "dp"), "tensor"),
            P(None, "tensor"),
            P(None, "tensor"),
            P("tensor", None),
            P("groups", "tensor", None),
            P("groups", None, "tensor"),
            P(("groups", "dp")),
            P("groups"),
        ),
        out_specs=(
            P(("groups", "dp"), "tensor"),
            P("groups", "tensor", None),
            P("groups", None, "tensor"),
        ),
        check_vma=False,
    )
```
